32 devices in a mesh: beam: 2 (over y), freq: 8 (over z, x), tm: 2 (over core).
Axes of the slice: x: 2, y: 2, z: 4, core: 2. Of those that a mesh axis runs over, the one named last changes fastest.
Arguments:
- voltages: bfloat16 [4, 8192, 1024], P('beam', 'tm', 'freq'), parts along dimension 0, may hold values from -6 to 6
- pfb_taps: float32 [16, 128], replicated, may hold values from -1.5 to 1.5
- local_shift: int32 [7, 512], P(None, 'freq'), may hold values from 0 to 7
- cross_shift: int32 [3, 64], P(None, 'freq'), may hold values from 0 to 31, as said below
- tap_index: int32 [32, 128], replicated, may hold values from 0 to 255
- tap_weight: float32 [32, 128], replicated, may hold values from -0.5 to 0.5
Outputs:
- dedispersed: float32 [128, 8192], P(('beam', 'freq'), 'tm'), parts along dimension 0
- scores: float32 [128, 32, 256], P(('beam', 'freq'), None, 'tm'), parts along dimension 0
The draws below stay inside these ranges and needn't reach their ends.
There are 2 independent parts, one for each index of `beam`. The reference program is written for one: setup_inputs(seed, part) draws one part's arguments, and reference() takes and returns one part's arrays. A program takes and returns all parts, laid end to end along the dimension named above; an argument that names none is the same for every part. Nothing has to cross between parts.
Inputs may be any that keep to these rules, and one draw needn't show every extreme that they name: `cross_shift`: row j holds values 0 to 8 * 2**j - 1, and reaches that value.
All inputs are finite; a program needn't handle non-finite values.
Results may differ from the reference program's by a relative error of at most 0.0003.
Values may be sent and summed in bfloat16 or wider, within the bound.
No kernel may reach another device: no remote copies, remote signals or barrier semaphores. Data moves between devices by JAX's collectives and lax.ppermute only.
A program may use at most 64 MiB of HBM per device.

```python
import math
import jax
import jax.numpy as jnp
from jax import lax

CH_DEV = 128
TRIAL_DEV = 8
PFB_TAPS = 16
LSHIFT = 8
TEMPLATES = 32
TPL_TAPS = 128
STRIDE = 32
WIN = 256
LLEVELS = 7
XLEVELS = 3
CHANNELS = 1024
TRIALS = 64
FRAMES = 8192
N_FREQ = 8


def draw_cross_shift(key, part):
    first_key, second_key = jax.random.split(jax.random.fold_in(key, 17))
    raw_bits = jax.random.randint(first_key, (XLEVELS, TRIALS), 0, 1 << 20)
    limits = TRIAL_DEV * 2 ** jnp.arange(XLEVELS, dtype=jnp.int32)
    values = raw_bits % limits[:, None]
    peak_spot = jax.random.randint(second_key, (XLEVELS, 1), 0, TRIALS)
    column_ids = jnp.arange(TRIALS, dtype=jnp.int32)[None, :]
    return jnp.where(column_ids == peak_spot, limits[:, None] - 1, values).astype(jnp.int32)


def with_ends(values, stream_key, low, largest):
    dims = values.shape
    place = [jax.random.randint(jax.random.fold_in(stream_key, axis), (), 0, dims[axis]) for axis in range(len(dims))]
    values = values.at[tuple(place)].set(low)
    longest = dims.index(max(dims))
    place[longest] = (place[longest] + 1) % dims[longest]
    return values.at[tuple(place)].set(largest)


def levels(rng, extent, shards, low, high):
    level, own = 1.0, jax.random.fold_in(rng, 6)
    for position, blocks in shards:
        draws = jnp.exp(jax.random.uniform(jax.random.fold_in(own, position), (blocks,), jnp.float32, low / len(shards), high / len(shards)))
        level = level * jnp.repeat(draws, extent[position] // blocks).reshape([-1 if axis == position else 1 for axis in range(len(extent))])
    return level


def centred(rng, extent, width, most, pieces=(), held_as=jnp.bfloat16):
    drawn = width * jax.random.normal(rng, extent, jnp.float32)
    if pieces:
        drawn = drawn * levels(rng, extent, pieces, -0.22, 0.18)
    return jnp.clip(drawn, -most, most).astype(held_as)


def setup_inputs(seed: int = 0, part: int = 0) -> dict:
    splits = jax.random.split(jax.random.key(seed), 7)
    part_keys = jax.random.split(jax.random.fold_in(splits[6], part), 7)
    return {
        "voltages": centred(part_keys[0], (2, FRAMES, CHANNELS), 1.0, 6.0, ((1, 2), (2, 8))),
        "pfb_taps": centred(splits[1], (PFB_TAPS, CH_DEV), 0.25, 1.5, (), jnp.float32),
        "local_shift": with_ends(jax.random.randint(splits[2], (LLEVELS, CHANNELS // 2), 0, LSHIFT), jax.random.fold_in(splits[2], 1), 0, LSHIFT - 1).astype(jnp.int32),
        "cross_shift": draw_cross_shift(jax.random.fold_in(splits[6], 71), part),
        "tap_index": with_ends(jax.random.randint(splits[4], (TEMPLATES, TPL_TAPS), 0, WIN), jax.random.fold_in(splits[4], 1), 0, WIN - 1).astype(jnp.int32),
        "tap_weight": centred(splits[5], (TEMPLATES, TPL_TAPS), TPL_TAPS ** -0.5, 0.5, (), jnp.float32),
    }


def filter_taps(padded, pfb_taps, length):

    def add_tap(tap_step, running):
        sliced = lax.dynamic_slice_in_dim(padded, PFB_TAPS - 1 - tap_step, length, axis=1)
        weight = lax.dynamic_index_in_dim(pfb_taps, tap_step, 0, keepdims=False)
        return running + sliced * weight
    shape_zero = jnp.zeros((2, length, padded.shape[2]), jnp.float32)
    return lax.fori_loop(0, PFB_TAPS, add_tap, shape_zero)

def delayed(source, shifts, offset, length):
    frame_ids = jnp.arange(length, dtype=jnp.int32)
    lookup = offset + frame_ids - shifts[..., None].astype(jnp.int32)
    inside = lookup >= 0
    picked = jnp.take_along_axis(source, jnp.maximum(lookup, 0), axis=-1)
    return jnp.where(inside, picked, jnp.zeros_like(picked))

def merge_pairs(series, shifts, trials):
    paired = series.reshape(series.shape[0] // 2, 2, series.shape[1], series.shape[2])
    leading = paired[:, 0]
    trailing = paired[:, 1]
    if trials > series.shape[1]:
        leading = jnp.concatenate([leading, leading], axis=1)
        trailing = jnp.concatenate([trailing, trailing], axis=1)
    return leading + delayed(trailing, shifts, 0, series.shape[2])

def local_fdmt(powers, shift_table):
    series = powers[:, None, :]
    for level_index in range(1, LLEVELS + 1):
        trials = max(1, TRIAL_DEV * 2 ** level_index // CH_DEV)
        band_count = CH_DEV // 2 ** level_index
        shifts = shift_table[level_index - 1].reshape(band_count, 2 ** (level_index - 1))[:, :trials]
        series = merge_pairs(series, shifts, trials)
    return series[0]

def band_power(band_volts, pfb_taps):
    frame_count = band_volts.shape[1]
    padded = jnp.pad(band_volts.astype(jnp.float32), ((0, 0), (PFB_TAPS - 1, 0), (0, 0)))
    filtered = filter_taps(padded, pfb_taps, frame_count)
    spectrum = jnp.fft.fft(filtered[0] + 1j * filtered[1], axis=-1)
    powers = (jnp.real(spectrum) ** 2 + jnp.imag(spectrum) ** 2) / CH_DEV
    powers = powers.T
    return powers - lax.optimization_barrier(jnp.mean(powers, axis=1, keepdims=True))

def template_matrix(tap_index, tap_weight):
    matches = (tap_index[:, :, None] == jnp.arange(WIN, dtype=jnp.int32)[None, None, :]).astype(jnp.float32)
    return jnp.einsum('nik,ni->nk', matches, tap_weight.astype(jnp.float32), precision=lax.Precision.HIGHEST)

def correlate(extended, matrix, positions):
    blocks = extended.reshape(extended.shape[0], -1, STRIDE)
    running = jnp.zeros((extended.shape[0], matrix.shape[0], positions), jnp.float32)
    for block_step in range(WIN // STRIDE):
        running = running + jnp.einsum('rjs,ns->rnj', blocks[:, block_step:block_step + positions], matrix[:, block_step * STRIDE:(block_step + 1) * STRIDE], precision=lax.Precision.HIGHEST)
    return running

def reference(voltages, pfb_taps, local_shift, cross_shift, tap_index, tap_weight):
    frame_count = voltages.shape[1]
    band_volts = voltages.reshape(2, frame_count, N_FREQ, CH_DEV).transpose(2, 0, 1, 3)
    band_tables = local_shift.reshape(LLEVELS, N_FREQ, CH_DEV // 2).transpose(1, 0, 2)

    def one_band(band_item):
        return local_fdmt(band_power(band_item[0], pfb_taps), band_item[1])
    series = lax.map(one_band, (band_volts, band_tables))
    for level_index in range(XLEVELS):
        trials = TRIAL_DEV * 2 ** (level_index + 1)
        shifts = cross_shift[level_index].reshape(N_FREQ // 2 ** (level_index + 1), trials)
        series = merge_pairs(series, shifts, trials)
    dedispersed = series[0] * (1.0 / math.sqrt(CHANNELS))
    extended = jnp.pad(dedispersed, ((0, 0), (0, WIN - STRIDE)))
    matrix = template_matrix(tap_index, tap_weight)
    scores = correlate(extended, matrix, frame_count // STRIDE)
    return (dedispersed, scores)
```

```python
import math

import jax
import jax.numpy as jnp
import numpy as np
from jax import lax
from jax.experimental import pallas as pl
from jax.experimental.pallas import tpu as pltpu
from jax.sharding import PartitionSpec as P

LSHIFT = 8
STRIDE = 32
WIN = 256
LANES = 128
ROWS = 8
BF = jnp.bfloat16
F32 = jnp.float32
NT = (((1,), (1,)), ((), ()))
VMEM = pl.BlockSpec(memory_space=pltpu.VMEM)
SMEM = pl.BlockSpec(memory_space=pltpu.SMEM)
PARAMS = pltpu.CompilerParams(vmem_limit_bytes=48 * 1024 * 1024)


def round_up(value, multiple):
    return -(-value // multiple) * multiple


def tile(k):
    return slice(k * LANES, (k + 1) * LANES)


def split(x):
    high = x.astype(BF)
    return high, (x - high.astype(F32)).astype(BF)


def lanes():
    return lax.broadcasted_iota(jnp.int32, (ROWS, LANES), 1)


def rotated(x, index):
    return jnp.take_along_axis(x, index, axis=1, mode="promise_in_bounds")


def merged(leading, trailing, shifts):
    lane = lanes()
    index = (lane - shifts) & (LANES - 1)
    inside = lane >= shifts
    before = jnp.zeros((ROWS, LANES), F32)
    out = []
    for lead, trail in zip(leading, trailing):
        turned = rotated(trail, index)
        out.append(lead + jnp.where(inside, turned, before))
        before = turned
    return out


def dft_table(channels, group):
    place = np.arange(channels)
    number = (place % (channels // group)) * group + place // (channels // group)
    phase = (number[:, None] * np.arange(channels)[None, :]) % channels
    angle = phase * (2.0 * np.pi / channels)
    cosine, sine = np.cos(angle), np.sin(angle)
    table = np.block([[cosine, sine], [-sine, cosine]])
    high = table.astype(np.float32).astype(jnp.bfloat16)
    low = (table - high.astype(np.float64)).astype(np.float32).astype(jnp.bfloat16)
    return np.concatenate([high, high, low], axis=1)


def shift_pickers(channels, group, level_count, columns):
    single = np.zeros((group.bit_length() - 1, channels, columns), np.float32)
    for row in range(channels):
        number = (row % (channels // group)) * group + row // (channels // group)
        for level in range(1, group.bit_length()):
            if number >> (level - 1) & 1:
                single[level - 1, row, (number >> level) << (level - 1)] = 1.0
    several = np.zeros((level_count - group.bit_length() + 1, ROWS, columns), np.float32)
    for step in range(several.shape[0]):
        level = group.bit_length() + step
        trials = 2 ** (step + 1)
        for row in range(ROWS):
            several[step, row, (row // trials) * 2 ** (level - 1) + row % trials] = 1.0
    return single, several


def spread_table(tiles, blocks):
    trials = LANES // tiles
    table = np.zeros((blocks, trials, tiles, trials, tiles * blocks), np.float32)
    for block in range(blocks):
        for trial in range(trials):
            for number in range(tiles):
                table[block, trial, number, trial, number * blocks + block] = 1.0
    return table.reshape(blocks * LANES, -1).astype(jnp.bfloat16)


def front_kernel(sizes, info, volts, halo, taps, table, single, several, shifts, out, samples, filtered, series, earlier, sums):
    frames, lead, tail, chunk_tiles = sizes
    channels = volts.shape[2]
    tap_count = taps.shape[0]
    groups = channels // ROWS
    margin = round_up(tap_count, 16)
    halo_rows = halo.shape[1]
    first, last = info[0] == 0, info[1] == 1

    for part in range(2):
        before = halo[part, halo_rows - lead - margin :, :].astype(F32)
        samples[part, : lead + margin, :] = jnp.where(first, 0.0, before)
        after = halo[part, :tail, :].astype(F32)
        samples[part, lead + margin + frames :, :] = jnp.where(last, 0.0, after)
    step_rows = 256

    def convert(step, carry):
        at = pl.multiple_of(step * step_rows, step_rows)
        for part in range(2):
            samples[part, pl.ds(at + lead + margin, step_rows), :] = volts[part, pl.ds(at, step_rows), :].astype(F32)
        return carry

    lax.fori_loop(0, frames // step_rows, convert, 0)

    def picked(pickers, level):
        row = jnp.broadcast_to(shifts[level : level + 1, :].astype(F32), (LANES, shifts.shape[1]))
        return lax.dot_general(pickers, row, NT, preferred_element_type=F32)

    total = picked(single[0], 0)
    for level in range(1, single.shape[0]):
        total = total + picked(single[level], level)
    total = total.astype(jnp.int32)
    lane = lanes()
    earlier[...] = jnp.zeros_like(earlier)
    sums[...] = jnp.zeros_like(sums)
    chunk = chunk_tiles * LANES
    stride = LANES // ROWS
    lead_tiles, main_tiles = lead // LANES, frames // LANES

    def one_chunk(number, carry):
        base = pl.multiple_of(number * chunk, LANES)
        for sub in range(chunk_tiles):
            for part in range(2):
                window = [
                    samples[part, pl.ds(base + sub * LANES + margin + m, ROWS, stride=stride), :]
                    for m in range(1 - tap_count, stride)
                ]
                for m in range(stride):
                    value = window[m + tap_count - 1] * taps[0:1, :]
                    for k in range(1, tap_count):
                        value = value + window[m + tap_count - 1 - k] * taps[k : k + 1, :]
                    filtered[part, pl.ds(sub * LANES + m, ROWS, stride=stride), :] = value
        real_high, real_low = split(filtered[0])
        imag_high, imag_low = split(filtered[1])
        operand = jnp.concatenate([real_high, imag_high, real_low, imag_low, real_high, imag_high], axis=1)
        spectrum = lax.dot_general(table[...], operand, NT, preferred_element_type=F32)
        power = spectrum[:channels] * spectrum[channels:]
        power = spectrum[:channels] * spectrum[:channels] + spectrum[channels:] * spectrum[channels:]
        for sub in range(chunk_tiles):
            place = number * chunk_tiles + sub
            counted = jnp.logical_and(place >= lead_tiles, place < lead_tiles + main_tiles)
            acc = jnp.zeros((ROWS, LANES), F32)
            for j in range(groups):
                rows = slice(j * ROWS, (j + 1) * ROWS)
                shift = total[rows]
                value = power[rows, tile(sub)]
                turned = rotated(value, (lane - shift) & (LANES - 1))
                acc = acc + jnp.where(lane >= shift, turned, earlier[rows])
                earlier[rows] = turned
                sums[rows] += jnp.where(counted, value, 0.0)
            series[:, pl.ds(pl.multiple_of(lead + base + sub * LANES, LANES), LANES)] = acc
        return carry

    lax.fori_loop(0, (lead + frames + tail) // chunk, one_chunk, 0)

    settled = jnp.zeros((ROWS, LANES), F32)
    begun = jnp.zeros((ROWS, LANES), F32)
    for j in range(groups):
        rows = slice(j * ROWS, (j + 1) * ROWS)
        channel_sum = jnp.broadcast_to(jnp.sum(sums[rows], axis=1, keepdims=True), (ROWS, LANES))
        settled = settled + channel_sum
        begun = begun + jnp.where(lane >= total[rows], channel_sum, 0.0)
    series[:, :LANES] = begun
    for k in range(1, lead_tiles):
        series[:, tile(k)] = settled

    tiles = [series[:, tile(k)] for k in range(series.shape[1] // LANES)]
    row = lax.broadcasted_iota(jnp.int32, (ROWS, LANES), 0)
    for step in range(several.shape[0]):
        distance = 2**step
        upper = (row // distance) % 2 == 1
        leading = [jnp.where(upper, pltpu.roll(x, distance, 0), x) for x in tiles]
        trailing = [jnp.where(upper, x, pltpu.roll(x, ROWS - distance, 0)) for x in tiles]
        tiles = merged(leading, trailing, picked(several[step], single.shape[0] + step).astype(jnp.int32))
    for k, x in enumerate(tiles):
        out[:, tile(k)] = x


def ordered(own, partner, is_upper):
    count = own.shape[1] // LANES
    mine = [own[:, tile(k)] for k in range(count)]
    theirs = [partner[:, tile(k)] for k in range(count)]
    leading = [jnp.where(is_upper, y, x) for x, y in zip(mine, theirs)]
    trailing = [jnp.where(is_upper, x, y) for x, y in zip(mine, theirs)]
    return leading, trailing


def merge_kernel(level, info, own, partner, shifts, out):
    leading, trailing = ordered(own, partner, info[2 + level] == 1)
    for k, x in enumerate(merged(leading, trailing, shifts[level])):
        out[:, tile(k)] = x


def back_kernel(level, sizes, info, own, partner, other, across, shifts, weights, spread, dedispersed, scores, steps):
    frames, lead, tail, factor, window_count, stations = sizes
    first, last = info[0] == 0, info[1] == 1
    lead_tiles, main_tiles, tail_tiles = lead // LANES, frames // LANES, tail // LANES
    if level is None:
        series = [own[:, tile(k)] for k in range(own.shape[1] // LANES)]
        beside = [other[:, tile(k)] for k in range(lead_tiles)]
    else:
        is_upper = info[2 + level] == 1
        series = merged(*ordered(own, partner, is_upper), shifts[level])
        beside = merged(*ordered(other, across, is_upper), shifts[level])
    means = [(series[k] + beside[k]) * (1.0 / window_count) for k in range(lead_tiles)]
    settled = jnp.broadcast_to(means[-1][:, LANES - 1 :], (ROWS, LANES))
    for k in range(main_tiles + tail_tiles):
        mean = jnp.where(first, means[k], settled) if k < lead_tiles else settled
        value = (series[2 * lead_tiles + k] - mean) * factor
        if k < main_tiles:
            dedispersed[:, tile(k)] = value
        else:
            value = jnp.where(last, 0.0, value)
        steps[k * ROWS : (k + 1) * ROWS, :] = value

    reach = tail_tiles + 1
    parts = []
    for q in range(reach):
        parts.append(
            jnp.concatenate([steps[pl.ds(d + ROWS * q, main_tiles, stride=ROWS), :] for d in range(ROWS)], axis=0)
        )
    operand = jnp.concatenate(parts, axis=1)
    high, low = split(operand)
    weight_high, weight_low = split(weights[...])
    product = lax.dot_general(
        jnp.concatenate([weight_high, weight_high, weight_low], axis=1),
        jnp.concatenate([high, low, high], axis=1),
        NT,
        preferred_element_type=F32,
    )
    blocks = LANES // STRIDE
    templates = product.shape[0] // blocks
    sets = product.shape[1] // LANES
    grouped = jnp.concatenate(
        [
            jnp.concatenate([product[i * templates : (i + 1) * templates, tile(a)] for i in range(blocks)], axis=1)
            for a in range(sets)
        ],
        axis=0,
    )
    one = grouped.astype(BF)
    rest = grouped - one.astype(F32)
    two = rest.astype(BF)
    three = (rest - two.astype(F32)).astype(BF)
    placed = jnp.dot(jnp.concatenate([one, two, three], axis=0), spread[...], preferred_element_type=F32)
    count = sets * templates
    placed = placed[:count] + placed[count : 2 * count] + placed[2 * count :]
    trials = LANES // main_tiles
    positions = main_tiles * blocks
    for a in range(sets):
        for d in range(trials):
            scores[a * trials + d] = placed[a * templates : (a + 1) * templates, d * positions : (d + 1) * positions]


def swapped(x, axis, distance):
    return lax.ppermute(x, axis, [(i, i ^ distance) for i in range(lax.axis_size(axis))])


def template_weights(tap_index, tap_weight, reach):
    hit = tap_index[:, :, None] == jnp.arange(WIN, dtype=jnp.int32)[None, None, :]
    template = jnp.sum(jnp.where(hit, tap_weight[:, :, None], 0.0), axis=1)
    width = reach * LANES
    rows = [
        jnp.pad(template, ((0, 0), (i * STRIDE, width - WIN - i * STRIDE))) for i in range(LANES // STRIDE)
    ]
    return jnp.concatenate(rows, axis=0)


def wide_merge(own, partner, is_upper, shifts):
    leading = jnp.where(is_upper, partner, own)
    trailing = jnp.where(is_upper, own, partner)
    place = jnp.arange(own.shape[1], dtype=jnp.int32)[None, :] - shifts[:, None]
    picked = jnp.take_along_axis(trailing, jnp.maximum(place, 0), axis=1)
    return leading + jnp.where(place >= 0, picked, 0.0)


def on_device(voltages, pfb_taps, local_shift, cross_shift, tap_index, tap_weight):
    frames, channels = voltages.shape[1:]
    tap_count = pfb_taps.shape[0]
    trials = cross_shift.shape[1]
    local_levels = local_shift.shape[0]
    tm_size, freq_size = lax.axis_size("tm"), lax.axis_size("freq")
    levels = freq_size.bit_length() - 1
    group = channels // trials
    margin = round_up(tap_count, 16)
    cross_reach = sum(trials * 2**level - 1 for level in range(levels))
    lead = round_up(local_levels * (LSHIFT - 1) + cross_reach, LANES)
    tail = round_up(WIN - STRIDE, LANES)

    time, freq = lax.axis_index("tm"), lax.axis_index("freq")
    info = jnp.stack(
        [time, (time == tm_size - 1).astype(jnp.int32)] + [freq >> level & 1 for level in range(max(levels, 1))]
    ).astype(jnp.int32)
    halo_rows = round_up(max(lead + margin, tail), 16)
    if tm_size == 2:
        sent = jnp.where(time == 0, voltages[:, frames - halo_rows :], voltages[:, :halo_rows])
        halo = swapped(sent, "tm", 1)
    else:
        raise NotImplementedError("tm")

    total_tiles = (lead + frames + tail) // LANES
    chunk_tiles = max(m for m in range(1, 6) if total_tiles % m == 0)
    table = jnp.asarray(dft_table(channels, group))
    single, several = (jnp.asarray(x) for x in shift_pickers(channels, group, local_levels, local_shift.shape[1]))
    width = 2 * lead + frames + tail
    ext = lead + frames + tail

    def front(*refs):
        front_kernel((frames, lead, tail, chunk_tiles), *refs)

    series = pl.pallas_call(
        front,
        out_shape=jax.ShapeDtypeStruct((trials, width), F32),
        in_specs=[SMEM] + [VMEM] * 7,
        out_specs=VMEM,
        scratch_shapes=[
            pltpu.VMEM((2, margin + ext, channels), F32),
            pltpu.VMEM((2, chunk_tiles * LANES, channels), F32),
            pltpu.VMEM((trials, width), F32),
            pltpu.VMEM((channels, LANES), F32),
            pltpu.VMEM((channels, LANES), F32),
        ],
        compiler_params=PARAMS,
        name="front",
    )(info, voltages, halo, pfb_taps, table, single, several, local_shift)

    shift_rows = jnp.broadcast_to(cross_shift[:, :, None], cross_shift.shape + (LANES,))
    fused = levels > 0 and trials * 2 ** (levels - 1) <= LANES
    for level in range(levels - 1 if fused else levels):
        partner = swapped(series, "freq", 2**level)
        if trials * 2**level <= LANES:

            def merge(*refs, level=level):
                merge_kernel(level, *refs)

            series = pl.pallas_call(
                merge,
                out_shape=jax.ShapeDtypeStruct(series.shape, F32),
                in_specs=[SMEM] + [VMEM] * 3,
                out_specs=VMEM,
                compiler_params=PARAMS,
                name="merge",
            )(info, series, partner, shift_rows)
        else:
            series = wide_merge(series, partner, info[2 + level] == 1, cross_shift[level])

    own_response = series[:, :lead]
    other = swapped(own_response, "tm", 1)
    if fused:
        last_level = levels - 1
        partner = swapped(series, "freq", 2**last_level)
        pairs = [
            (f * tm_size + t, (f ^ 2**last_level) * tm_size + (t ^ 1))
            for f in range(freq_size)
            for t in range(tm_size)
        ]
        across = lax.ppermute(own_response, ("freq", "tm"), pairs)
    else:
        last_level, partner, across = None, series, other

    weights = template_weights(tap_index, tap_weight, tail // LANES + 1)
    templates = tap_index.shape[0]
    spread = jnp.asarray(spread_table(frames // LANES, LANES // STRIDE))
    factor = 1.0 / (channels * math.sqrt(channels * freq_size))

    def back(*refs):
        back_kernel(last_level, (frames, lead, tail, factor, frames * tm_size, STRIDE), *refs)

    return pl.pallas_call(
        back,
        out_shape=(
            jax.ShapeDtypeStruct((trials, frames), F32),
            jax.ShapeDtypeStruct((trials, templates, frames // STRIDE), F32),
        ),
        in_specs=[SMEM] + [VMEM] * 7,
        out_specs=(VMEM, VMEM),
        scratch_shapes=[pltpu.VMEM(((frames + tail) // LANES * ROWS, LANES), F32)],
        compiler_params=PARAMS,
        name="back",
    )(info, series, partner, other, across, shift_rows, weights, spread)


def solution(mesh):
    return jax.shard_map(
        on_device,
        mesh=mesh,
        in_specs=(P("beam", "tm", "freq"), P(), P(None, "freq"), P(None, "freq"), P(), P()),
        out_specs=(P(("beam", "freq"), "tm"), P(("beam", "freq"), None, "tm")),
        check_vma=False,
    )
```

```python
import math

import jax
import jax.numpy as jnp
import numpy as np
from jax import lax
from jax.experimental import pallas as pl
from jax.experimental.pallas import tpu as pltpu
from jax.sharding import PartitionSpec as P

LSHIFT = 8
STRIDE = 32
WIN = 256
SET = 5
LARGEST = 32000.0
LANES = 128
ROWS = 8
BF = jnp.bfloat16
F32 = jnp.float32
NT = (((1,), (1,)), ((), ()))
VMEM = pl.BlockSpec(memory_space=pltpu.VMEM)
SMEM = pl.BlockSpec(memory_space=pltpu.SMEM)
ANY = pl.BlockSpec(memory_space=pl.ANY)
PARAMS = pltpu.CompilerParams(vmem_limit_bytes=48 * 1024 * 1024)


def round_up(value, multiple):
    return -(-value // multiple) * multiple


def whole(array):
    return pl.BlockSpec(array.shape, lambda *_: (0,) * array.ndim)


def tile(k):
    return slice(k * LANES, (k + 1) * LANES)


def split(x):
    high = x.astype(BF)
    return high, (x - high.astype(F32)).astype(BF)


def lanes():
    return lax.broadcasted_iota(jnp.int32, (ROWS, LANES), 1)


def rotated(x, index):
    return jnp.take_along_axis(x, index, axis=1, mode="promise_in_bounds")


def merged(leading, trailing, shifts, lead_tiles):
    lane = lanes()
    index = (lane - shifts) & (LANES - 1)
    inside = lane >= shifts
    out = []
    for k, (lead, trail) in enumerate(zip(leading, trailing)):
        if k in (0, lead_tiles):
            before = jnp.zeros((ROWS, LANES), F32)
        turned = rotated(trail, index)
        out.append(lead + jnp.where(inside, turned, before))
        before = turned
    return out


def dft_table(channels, group):
    place = np.arange(channels)
    number = (place % (channels // group)) * group + place // (channels // group)
    phase = (np.arange(channels)[:, None] * number[None, :]) % channels
    angle = phase * (2.0 * np.pi / channels)
    cosine, sine = np.cos(angle), np.sin(angle)
    return np.block([[cosine, -sine], [sine, cosine]]).astype(np.float32)


def spread_table(tiles, blocks):
    trials = LANES // tiles
    table = np.zeros((blocks, trials, tiles, trials, tiles * blocks), np.float32)
    for block in range(blocks):
        for trial in range(trials):
            for number in range(tiles):
                table[block, trial, number, trial, number * blocks + block] = 1.0
    return table.reshape(blocks * LANES, -1).astype(jnp.bfloat16)


def front_kernel(
    sizes, info, volts, beside, packed, out, words, notes, held, samples, *scratch
):
    filtered, spectra = (scratch[:2], scratch[2:4]), scratch[4:6]
    series, sums, arrived = scratch[6:]
    frames, lead, tail, chunk_tiles, pieces, tap_count, level_count, columns = sizes
    channels = volts.shape[2]
    taps_at, shifts_at = 2 * channels, 2 * channels + tap_count
    group_count = channels // ROWS
    margin = round_up(tap_count, 16)
    halo_rows = beside.shape[1]
    first, last = info[0] == 0, info[1] == 1
    piece = frames // pieces

    def copies(number):
        rows = slice(number * piece, (number + 1) * piece)
        return pltpu.make_async_copy(volts.at[:, rows, :], held.at[:, rows, :], arrived.at[number])

    copies(0).start()
    for number in range(1, pieces):
        copies(number).start()

    place = lax.broadcasted_iota(jnp.int32, (channels, columns), 0)
    column = lax.broadcasted_iota(jnp.int32, (channels, columns), 1)
    channel = (place & (ROWS - 1)) * group_count + (place >> (ROWS.bit_length() - 1))
    single_levels = group_count.bit_length() - 1

    def picked(hit, level):
        row = jnp.broadcast_to(packed[shifts_at + level : shifts_at + level + 1, :columns], (LANES, columns))
        return lax.dot_general(hit.astype(F32), row, NT, preferred_element_type=F32)

    total = jnp.zeros((channels, LANES), F32)
    for level in range(single_levels):
        trailing = (channel >> level & 1) == 1
        spot = (channel >> (level + 1)) << level
        total = total + picked(jnp.logical_and(trailing, column == spot), level)
    total = total.astype(jnp.int32)
    shift = [total[j * ROWS : (j + 1) * ROWS] for j in range(group_count)]
    lane = lanes()
    lead_tiles, main_tiles, tail_tiles = lead // LANES, frames // LANES, tail // LANES
    tile_count = lead_tiles + main_tiles + tail_tiles

    def convert(number):
        if number == pieces:
            for part in range(2):
                before = beside[part, halo_rows - lead - margin :, :].astype(F32)
                samples[part, : lead + margin, :] = jnp.where(first, 0.0, before)
                after = beside[part, :tail, :].astype(F32)
                samples[part, lead + margin + frames :, :] = jnp.where(last, 0.0, after)
            return
        copies(number).wait()
        rows = slice(number * piece, (number + 1) * piece)
        at = lead + margin + number * piece
        for part in range(2):
            samples[part, at : at + piece, :] = held[part, rows, :].astype(F32)

    def filter_tile(number, into):
        for part in range(2):
            base = number * LANES + margin
            value = samples[part, base : base + LANES, :] * packed[taps_at : taps_at + 1, :channels]
            for k in range(1, tap_count):
                value = value + samples[part, base - k : base - k + LANES, :] * packed[taps_at + k : taps_at + k + 1, :channels]
            filtered[into[0]][part][into[1] * LANES : (into[1] + 1) * LANES, :] = value

    def transform(slot, count):
        rows = slice(0, count * LANES)
        both = jnp.concatenate([filtered[slot][0][rows, :], filtered[slot][1][rows, :]], axis=1)
        spectra[slot][rows, :] = jnp.dot(
            both, packed[:taps_at, :], preferred_element_type=F32, precision=lax.Precision.HIGH
        )

    def collapse_tile(number, slot, sub, earlier):
        real, imag = spectra[slot][tile(sub), :channels], spectra[slot][tile(sub), channels:]
        power = (real * real + imag * imag).T
        counted = lead_tiles <= number < lead_tiles + main_tiles
        acc = jnp.zeros((ROWS, LANES), F32)
        now = []
        for j in range(group_count):
            rows = slice(j * ROWS, (j + 1) * ROWS)
            value = power[rows]
            turned = rotated(value, (lane - shift[j]) & (LANES - 1))
            acc = acc + jnp.where(lane >= shift[j], turned, earlier[j])
            now.append(turned)
            if counted:
                sums[rows] += value
        series[:, tile(lead_tiles + number)] = acc
        return now

    sums[...] = jnp.zeros_like(sums)
    starts = list(range(0, tile_count, chunk_tiles)) + [tile_count]
    chunks = len(starts) - 1
    earlier = [jnp.zeros((ROWS, LANES), F32)] * group_count
    converted = 0
    convert(pieces)
    for step in range(chunks + 2):
        if step < chunks:
            needed = min(pieces, -(-((starts[step + 1] - lead_tiles) * LANES) // piece))
            while converted < needed:
                convert(converted)
                converted += 1
        if 1 <= step <= chunks:
            transform((step - 1) % 2, starts[step] - starts[step - 1])
        for sub in range(chunk_tiles):
            if step < chunks and starts[step] + sub < starts[step + 1]:
                filter_tile(starts[step] + sub, (step % 2, sub))
            if step >= 2 and starts[step - 2] + sub < starts[step - 1]:
                earlier = collapse_tile(starts[step - 2] + sub, step % 2, sub, earlier)

    settled = jnp.zeros((ROWS, LANES), F32)
    begun = jnp.zeros((ROWS, LANES), F32)
    for j in range(group_count):
        rows = slice(j * ROWS, (j + 1) * ROWS)
        channel_sum = jnp.broadcast_to(jnp.sum(sums[rows], axis=1, keepdims=True), (ROWS, LANES))
        settled = settled + channel_sum
        begun = begun + jnp.where(lane >= shift[j], channel_sum, 0.0)
    series[:, :LANES] = begun
    for k in range(1, lead_tiles):
        series[:, tile(k)] = settled

    tiles = [series[:, tile(k)] for k in range(lead_tiles + tile_count)]
    row = lax.broadcasted_iota(jnp.int32, (ROWS, LANES), 0)
    slot_row = lax.broadcasted_iota(jnp.int32, (ROWS, columns), 0)
    slot_column = lax.broadcasted_iota(jnp.int32, (ROWS, columns), 1)
    for step in range(level_count - single_levels):
        level = single_levels + step
        distance = 2**step
        upper = (row & distance) > 0
        leading = [jnp.where(upper, pltpu.roll(x, distance, 0), x) for x in tiles]
        trailing = [jnp.where(upper, x, pltpu.roll(x, ROWS - distance, 0)) for x in tiles]
        spot = ((slot_row >> (step + 1)) << level) + (slot_row & (2 * distance - 1))
        tiles = merged(leading, trailing, picked(slot_column == spot, level).astype(jnp.int32), lead_tiles)
    for k, x in enumerate(tiles):
        out[:, tile(k)] = x
    encode(tiles, lead_tiles, words, notes)


def pieces_of(count, lead_tiles):
    starts = [0] + list(range(lead_tiles, count, SET)) + [count]
    return [range(at, to) for at, to in zip(starts[:-1], starts[1:])]


def encode(tiles, lead_tiles, words, notes):
    lane = lanes()
    body = tiles[lead_tiles:]
    for k in range(lead_tiles):
        notes[:, tile(k)] = tiles[k]
    note = jnp.zeros((ROWS, LANES), F32)
    steps = []
    for number, members in enumerate(pieces_of(len(body), lead_tiles)):
        top, bottom = body[members[0]], body[members[0]]
        for k in members[1:]:
            top, bottom = jnp.maximum(top, body[k]), jnp.minimum(bottom, body[k])
        top = jnp.max(top, axis=1, keepdims=True)
        bottom = jnp.min(bottom, axis=1, keepdims=True)
        middle = 0.5 * top + 0.5 * bottom
        half = jnp.maximum(0.5 * top - 0.5 * bottom, 1e-30)
        note = jnp.where(lane == 2 * number, middle, note)
        note = jnp.where(lane == 2 * number + 1, half * (1.0 / LARGEST), note)
        per_step = jnp.broadcast_to(LARGEST / half, (ROWS, LANES))
        middle = jnp.broadcast_to(middle, (ROWS, LANES))
        steps.extend(jnp.floor((body[k] - middle) * per_step + 0.5) for k in members)
    notes[:, tile(lead_tiles)] = note
    if len(steps) % 2:
        steps.append(jnp.zeros((ROWS, LANES), F32))
    for k in range(len(steps) // 2):
        pair = jnp.concatenate([steps[2 * k], steps[2 * k + 1]], axis=0)
        words[:, tile(k)] = pair.astype(jnp.int32).astype(jnp.int16)


def decode(words, notes, count, lead_tiles):
    tiles = [notes[:, tile(k)] for k in range(lead_tiles)]
    note = notes[:, tile(lead_tiles)]
    steps = []
    for k in range(words.shape[1] // LANES):
        pair = words[:, tile(k)].astype(jnp.int32).astype(F32)
        steps += [pair[:ROWS], pair[ROWS:]]
    for number, members in enumerate(pieces_of(count - lead_tiles, lead_tiles)):
        middle = jnp.broadcast_to(note[:, 2 * number : 2 * number + 1], (ROWS, LANES))
        size = jnp.broadcast_to(note[:, 2 * number + 1 : 2 * number + 2], (ROWS, LANES))
        tiles.extend(steps[k] * size + middle for k in members)
    return tiles


def ordered(mine, theirs, is_upper):
    leading = [jnp.where(is_upper, y, x) for x, y in zip(mine, theirs)]
    trailing = [jnp.where(is_upper, x, y) for x, y in zip(mine, theirs)]
    return leading, trailing


def tiles_of(ref):
    return [ref[:, tile(k)] for k in range(ref.shape[1] // LANES)]


def merge_kernel(level, lead_tiles, info, own, words, notes, other, across, shifts, out, *sent):
    mine = tiles_of(own)
    theirs = decode(words, notes, len(mine), lead_tiles)
    if level == 0:
        for k in range(lead_tiles):
            mine[k], theirs[k] = mine[k] + other[:, tile(k)], theirs[k] + across[:, tile(k)]
    tiles = merged(*ordered(mine, theirs, info[2 + level] == 1), shifts[level], lead_tiles)
    for k, x in enumerate(tiles):
        out[:, tile(k)] = x
    if sent:
        encode(tiles, lead_tiles, *sent)


def back_kernel(level, sizes, info, own, words, notes, shifts, weights, spread, dedispersed, scores, steps):
    frames, lead, tail, factor, window_count, stations = sizes
    first, last = info[0] == 0, info[1] == 1
    lead_tiles, main_tiles, tail_tiles = lead // LANES, frames // LANES, tail // LANES
    if level is None:
        series = tiles_of(own)
    else:
        is_upper = info[2 + level] == 1
        mine = tiles_of(own)
        theirs = decode(words, notes, len(mine), lead_tiles)
        series = merged(*ordered(mine, theirs, is_upper), shifts[level], lead_tiles)
    means = [series[k] * (1.0 / window_count) for k in range(lead_tiles)]
    settled = jnp.broadcast_to(means[-1][:, LANES - 1 :], (ROWS, LANES))
    for k in range(main_tiles + tail_tiles):
        mean = jnp.where(first, means[k], settled) if k < lead_tiles else settled
        value = (series[2 * lead_tiles + k] - mean) * factor
        if k < main_tiles:
            dedispersed[:, tile(k)] = value
        else:
            value = jnp.where(last, 0.0, value)
        steps[k * ROWS : (k + 1) * ROWS, :] = value

    reach = tail_tiles + 1
    parts = []
    for q in range(reach):
        parts.append(
            jnp.concatenate([steps[pl.ds(d + ROWS * q, main_tiles, stride=ROWS), :] for d in range(ROWS)], axis=0)
        )
    operand = jnp.concatenate(parts, axis=1)
    high, low = split(operand)
    weight_high, weight_low = split(weights[...])
    product = lax.dot_general(
        jnp.concatenate([weight_high, weight_high, weight_low], axis=1),
        jnp.concatenate([high, low, high], axis=1),
        NT,
        preferred_element_type=F32,
    )
    blocks = LANES // STRIDE
    templates = product.shape[0] // blocks
    sets = product.shape[1] // LANES
    grouped = jnp.concatenate(
        [
            jnp.concatenate([product[i * templates : (i + 1) * templates, tile(a)] for i in range(blocks)], axis=1)
            for a in range(sets)
        ],
        axis=0,
    )
    one = grouped.astype(BF)
    rest = grouped - one.astype(F32)
    two = rest.astype(BF)
    three = (rest - two.astype(F32)).astype(BF)
    placed = jnp.dot(jnp.concatenate([one, two, three], axis=0), spread[...], preferred_element_type=F32)
    count = sets * templates
    placed = placed[:count] + placed[count : 2 * count] + placed[2 * count :]
    trials = LANES // main_tiles
    positions = main_tiles * blocks
    for a in range(sets):
        for d in range(trials):
            scores[a * trials + d] = placed[a * templates : (a + 1) * templates, d * positions : (d + 1) * positions]


def swapped(x, axis, distance):
    return lax.ppermute(x, axis, [(i, i ^ distance) for i in range(lax.axis_size(axis))])


def template_weights(tap_index, tap_weight, reach):
    hit = tap_index[:, :, None] == jnp.arange(WIN, dtype=jnp.int32)[None, None, :]
    template = jnp.sum(jnp.where(hit, tap_weight[:, :, None], 0.0), axis=1)
    width = reach * LANES
    rows = [
        jnp.pad(template, ((0, 0), (i * STRIDE, width - WIN - i * STRIDE))) for i in range(LANES // STRIDE)
    ]
    return jnp.concatenate(rows, axis=0)


def wide_merge(own, partner, is_upper, shifts):
    leading = jnp.where(is_upper, partner, own)
    trailing = jnp.where(is_upper, own, partner)
    place = jnp.arange(own.shape[1], dtype=jnp.int32)[None, :] - shifts[:, None]
    picked = jnp.take_along_axis(trailing, jnp.maximum(place, 0), axis=1)
    return leading + jnp.where(place >= 0, picked, 0.0)


def on_device(voltages, pfb_taps, local_shift, cross_shift, tap_index, tap_weight):
    frames, channels = voltages.shape[1:]
    tap_count = pfb_taps.shape[0]
    trials = cross_shift.shape[1]
    local_levels = local_shift.shape[0]
    tm_size, freq_size = lax.axis_size("tm"), lax.axis_size("freq")
    levels = freq_size.bit_length() - 1
    group = channels // trials
    margin = round_up(tap_count, 16)
    cross_reach = sum(trials * 2**level - 1 for level in range(levels))
    lead = round_up(local_levels * (LSHIFT - 1) + cross_reach, LANES)
    tail = round_up(WIN - STRIDE, LANES)

    time, freq = lax.axis_index("tm"), lax.axis_index("freq")
    info = jnp.stack(
        [time, (time == tm_size - 1).astype(jnp.int32)] + [freq >> level & 1 for level in range(max(levels, 1))]
    ).astype(jnp.int32)
    halo_rows = round_up(max(lead + margin, tail), 16)
    if tm_size == 2:
        start = jnp.where(time == 0, frames - halo_rows, 0)
        sent = lax.dynamic_slice_in_dim(voltages, start, halo_rows, axis=1)
        halo = swapped(sent, "tm", 1)
    else:
        raise NotImplementedError("tm")

    chunk_tiles, pieces = 5, 8
    table = jnp.asarray(dft_table(channels, group))
    extended = lead + frames + tail
    width = lead + extended

    sizes = (frames, lead, tail, chunk_tiles, pieces, tap_count) + local_shift.shape
    wide = 2 * channels
    spare = ((0, -(tap_count + local_levels) % ROWS), (0, wide - local_shift.shape[1]))
    packed = jnp.concatenate(
        [table, jnp.pad(pfb_taps, ((0, 0), (0, wide - channels))), jnp.pad(local_shift.astype(F32), spare)], axis=0
    )

    def front(*refs):
        front_kernel(sizes, *refs)

    lead_tiles, body_tiles = lead // LANES, extended // LANES
    sent_shapes = (
        jax.ShapeDtypeStruct((2 * ROWS, -(-body_tiles // 2) * LANES), jnp.int16),
        jax.ShapeDtypeStruct((trials, lead + LANES), F32),
    )
    series_shape = jax.ShapeDtypeStruct((trials, width), F32)
    series, *sent = pl.pallas_call(
        front,
        out_shape=(series_shape,) + sent_shapes,
        in_specs=[SMEM, ANY, VMEM, VMEM],
        out_specs=(VMEM,) * 3,
        scratch_shapes=[
            pltpu.VMEM(voltages.shape, BF),
            pltpu.VMEM((2, margin + extended, channels), F32),
            *[pltpu.VMEM((chunk_tiles * LANES, channels), F32)] * 4,
            *[pltpu.VMEM((chunk_tiles * LANES, 2 * channels), F32)] * 2,
            pltpu.VMEM((trials, width), F32),
            pltpu.VMEM((channels, LANES), F32),
            pltpu.SemaphoreType.DMA((pieces,)),
        ],
        compiler_params=pltpu.CompilerParams(vmem_limit_bytes=52 * 1024 * 1024),
        cost_estimate=pl.CostEstimate(flops=2 * 10**10, bytes_accessed=4096, transcendentals=0),
        name="front",
    )(info, voltages, halo, packed)

    shift_rows = jnp.broadcast_to(cross_shift[:, :, None], cross_shift.shape + (LANES,))
    (tap_index, tap_weight), sent = lax.optimization_barrier(((tap_index, tap_weight), sent))
    weights = template_weights(tap_index, tap_weight, tail // LANES + 1)
    short = [level for level in range(levels) if trials * 2**level <= LANES]
    fused = len(short) == levels > 1
    other = swapped(sent[1][:, :lead], "tm", 1)
    for level in range(levels - 1 if fused else levels):
        if level in short:
            received = [swapped(x, "freq", 2**level) for x in sent]
            if level == 0:
                across = swapped(other, "freq", 1)
                received[0], weights = lax.optimization_barrier((received[0], weights))
            shapes = (series_shape,) + (sent_shapes if level + 1 in short else ())

            def merge(*refs, level=level):
                merge_kernel(level, lead_tiles, *refs)

            series, *sent = pl.pallas_call(
                merge,
                out_shape=shapes,
                in_specs=[SMEM] + [VMEM] * 6,
                out_specs=(VMEM,) * len(shapes),
                compiler_params=PARAMS,
                name="merge",
            )(info, series, *received, other, across, shift_rows)
        else:
            partner = swapped(series, "freq", 2**level)
            series = wide_merge(series, partner, info[2 + level] == 1, cross_shift[level])

    if fused:
        last_level = levels - 1
        received = [swapped(x, "freq", 2**last_level) for x in sent]
    else:
        last_level = None
        received = [other, other]

    templates = tap_index.shape[0]
    spread = jnp.asarray(spread_table(frames // LANES, LANES // STRIDE))
    factor = 1.0 / (channels * math.sqrt(channels * freq_size))

    def back(*refs):
        back_kernel(last_level, (frames, lead, tail, factor, frames * tm_size, STRIDE), *refs)

    return pl.pallas_call(
        back,
        out_shape=(
            jax.ShapeDtypeStruct((trials, frames), F32),
            jax.ShapeDtypeStruct((trials, templates, frames // STRIDE), F32),
        ),
        in_specs=[SMEM] + [VMEM] * 6,
        out_specs=(VMEM, VMEM),
        scratch_shapes=[pltpu.VMEM(((frames + tail) // LANES * ROWS, LANES), F32)],
        compiler_params=PARAMS,
        name="back",
    )(info, series, *received, shift_rows, weights, spread)


def solution(mesh):
    return jax.shard_map(
        on_device,
        mesh=mesh,
        in_specs=(P("beam", "tm", "freq"), P(), P(None, "freq"), P(None, "freq"), P(), P()),
        out_specs=(P(("beam", "freq"), "tm"), P(("beam", "freq"), None, "tm")),
        check_vma=False,
    )
```

```python
import math

import jax
import jax.numpy as jnp
import numpy as np
from jax import lax
from jax.experimental import pallas as pl
from jax.experimental.pallas import tpu as pltpu
from jax.sharding import PartitionSpec as P

LSHIFT = 8
STRIDE = 32
WIN = 256
SET = 5
LARGEST = 32000.0
LANES = 128
ROWS = 8
BF = jnp.bfloat16
F32 = jnp.float32
NT = (((1,), (1,)), ((), ()))
VMEM = pl.BlockSpec(memory_space=pltpu.VMEM)
SMEM = pl.BlockSpec(memory_space=pltpu.SMEM)
ANY = pl.BlockSpec(memory_space=pl.ANY)
PARAMS = pltpu.CompilerParams(vmem_limit_bytes=48 * 1024 * 1024)


def round_up(value, multiple):
    return -(-value // multiple) * multiple


def whole(array):
    return pl.BlockSpec(array.shape, lambda *_: (0,) * array.ndim)


def tile(k):
    return slice(k * LANES, (k + 1) * LANES)


def split(x):
    high = x.astype(BF)
    return high, (x - high.astype(F32)).astype(BF)


def lanes():
    return lax.broadcasted_iota(jnp.int32, (ROWS, LANES), 1)


def rotated(x, index):
    return jnp.take_along_axis(x, index, axis=1, mode="promise_in_bounds")


def merged(leading, trailing, shifts, lead_tiles):
    lane = lanes()
    index = (lane - shifts) & (LANES - 1)
    inside = lane >= shifts
    out = []
    for k, (lead, trail) in enumerate(zip(leading, trailing)):
        if k in (0, lead_tiles):
            before = jnp.zeros((ROWS, LANES), F32)
        turned = rotated(trail, index)
        out.append(lead + jnp.where(inside, turned, before))
        before = turned
    return out


def dft_table(channels, group):
    place = np.arange(channels)
    number = (place % (channels // group)) * group + place // (channels // group)
    phase = (np.arange(channels)[:, None] * number[None, :]) % channels
    angle = phase * (2.0 * np.pi / channels)
    cosine, sine = np.cos(angle), np.sin(angle)
    return np.block([[cosine, -sine], [sine, cosine]]).astype(np.float32)


def spread_table(tiles, blocks):
    trials = LANES // tiles
    table = np.zeros((blocks, trials, tiles, trials, tiles * blocks), np.float32)
    for block in range(blocks):
        for trial in range(trials):
            for number in range(tiles):
                table[block, trial, number, trial, number * blocks + block] = 1.0
    return table.reshape(blocks * LANES, -1).astype(jnp.bfloat16)


def front_kernel(
    sizes, info, volts, beside, packed, out, words, notes, held, samples, *scratch
):
    filtered, spectra = (scratch[:2], scratch[2:4]), scratch[4:6]
    series, sums, arrived = scratch[6:]
    frames, lead, tail, chunk_tiles, pieces, tap_count, level_count, columns = sizes
    channels = volts.shape[2]
    taps_at, shifts_at = 2 * channels, 2 * channels + tap_count
    group_count = channels // ROWS
    margin = round_up(tap_count, 16)
    halo_rows = beside.shape[1]
    first, last = info[0] == 0, info[1] == 1
    piece = frames // pieces

    def copies(number):
        rows = slice(number * piece, (number + 1) * piece)
        return pltpu.make_async_copy(volts.at[:, rows, :], held.at[:, rows, :], arrived.at[number])

    copies(0).start()
    for number in range(1, pieces):
        copies(number).start()

    place = lax.broadcasted_iota(jnp.int32, (channels, columns), 0)
    column = lax.broadcasted_iota(jnp.int32, (channels, columns), 1)
    channel = (place & (ROWS - 1)) * group_count + (place >> (ROWS.bit_length() - 1))
    single_levels = group_count.bit_length() - 1

    def picked(hit, level):
        row = jnp.broadcast_to(packed[shifts_at + level : shifts_at + level + 1, :columns], (LANES, columns))
        return lax.dot_general(hit.astype(F32), row, NT, preferred_element_type=F32)

    total = jnp.zeros((channels, LANES), F32)
    for level in range(single_levels):
        trailing = (channel >> level & 1) == 1
        spot = (channel >> (level + 1)) << level
        total = total + picked(jnp.logical_and(trailing, column == spot), level)
    total = total.astype(jnp.int32)
    shift = [total[j * ROWS : (j + 1) * ROWS] for j in range(group_count)]
    lane = lanes()
    lead_tiles, main_tiles, tail_tiles = lead // LANES, frames // LANES, tail // LANES
    tile_count = lead_tiles + main_tiles + tail_tiles

    def convert(number):
        if number == pieces:
            for part in range(2):
                before = beside[part, halo_rows - lead - margin :, :].astype(F32)
                samples[part, : lead + margin, :] = jnp.where(first, 0.0, before)
                after = beside[part, :tail, :].astype(F32)
                samples[part, lead + margin + frames :, :] = jnp.where(last, 0.0, after)
            return
        copies(number).wait()
        rows = slice(number * piece, (number + 1) * piece)
        at = lead + margin + number * piece
        for part in range(2):
            samples[part, at : at + piece, :] = held[part, rows, :].astype(F32)

    def filter_tile(number, into):
        for part in range(2):
            base = number * LANES + margin
            value = samples[part, base : base + LANES, :] * packed[taps_at : taps_at + 1, :channels]
            for k in range(1, tap_count):
                value = value + samples[part, base - k : base - k + LANES, :] * packed[taps_at + k : taps_at + k + 1, :channels]
            filtered[into[0]][part][into[1] * LANES : (into[1] + 1) * LANES, :] = value

    def transform(slot, count):
        rows = slice(0, count * LANES)
        both = jnp.concatenate([filtered[slot][0][rows, :], filtered[slot][1][rows, :]], axis=1)
        spectra[slot][rows, :] = jnp.dot(
            both, packed[:taps_at, :], preferred_element_type=F32, precision=lax.Precision.HIGH
        )

    def collapse_tile(number, slot, sub, earlier):
        real, imag = spectra[slot][tile(sub), :channels], spectra[slot][tile(sub), channels:]
        power = (real * real + imag * imag).T
        counted = lead_tiles <= number < lead_tiles + main_tiles
        acc = jnp.zeros((ROWS, LANES), F32)
        now = []
        for j in range(group_count):
            rows = slice(j * ROWS, (j + 1) * ROWS)
            value = power[rows]
            turned = rotated(value, (lane - shift[j]) & (LANES - 1))
            acc = acc + jnp.where(lane >= shift[j], turned, earlier[j])
            now.append(turned)
            if counted:
                sums[rows] += value
        series[:, tile(lead_tiles + number)] = acc
        return now

    sums[...] = jnp.zeros_like(sums)
    starts = list(range(0, tile_count, chunk_tiles)) + [tile_count]
    chunks = len(starts) - 1
    earlier = [jnp.zeros((ROWS, LANES), F32)] * group_count
    converted = 0
    convert(pieces)
    for step in range(chunks + 2):
        if step < chunks:
            needed = min(pieces, -(-((starts[step + 1] - lead_tiles) * LANES) // piece))
            while converted < needed:
                convert(converted)
                converted += 1
        if 1 <= step <= chunks:
            transform((step - 1) % 2, starts[step] - starts[step - 1])
        for sub in range(chunk_tiles):
            if step < chunks and starts[step] + sub < starts[step + 1]:
                filter_tile(starts[step] + sub, (step % 2, sub))
            if step >= 2 and starts[step - 2] + sub < starts[step - 1]:
                earlier = collapse_tile(starts[step - 2] + sub, step % 2, sub, earlier)

    settled = jnp.zeros((ROWS, LANES), F32)
    begun = jnp.zeros((ROWS, LANES), F32)
    for j in range(group_count):
        rows = slice(j * ROWS, (j + 1) * ROWS)
        channel_sum = jnp.broadcast_to(jnp.sum(sums[rows], axis=1, keepdims=True), (ROWS, LANES))
        settled = settled + channel_sum
        begun = begun + jnp.where(lane >= shift[j], channel_sum, 0.0)
    series[:, :LANES] = begun
    for k in range(1, lead_tiles):
        series[:, tile(k)] = settled

    tiles = [series[:, tile(k)] for k in range(lead_tiles + tile_count)]
    row = lax.broadcasted_iota(jnp.int32, (ROWS, LANES), 0)
    slot_row = lax.broadcasted_iota(jnp.int32, (ROWS, columns), 0)
    slot_column = lax.broadcasted_iota(jnp.int32, (ROWS, columns), 1)
    for step in range(level_count - single_levels):
        level = single_levels + step
        distance = 2**step
        upper = (row & distance) > 0
        leading = [jnp.where(upper, pltpu.roll(x, distance, 0), x) for x in tiles]
        trailing = [jnp.where(upper, x, pltpu.roll(x, ROWS - distance, 0)) for x in tiles]
        spot = ((slot_row >> (step + 1)) << level) + (slot_row & (2 * distance - 1))
        tiles = merged(leading, trailing, picked(slot_column == spot, level).astype(jnp.int32), lead_tiles)
    for k, x in enumerate(tiles):
        out[:, tile(k)] = x
    encode(tiles, lead_tiles, words, notes)


def pieces_of(count, lead_tiles):
    starts = [0] + list(range(lead_tiles, count, SET)) + [count]
    return [range(at, to) for at, to in zip(starts[:-1], starts[1:])]


def encode(tiles, lead_tiles, words, notes):
    lane = lanes()
    body = tiles[lead_tiles:]
    for k in range(lead_tiles):
        notes[:, tile(k)] = tiles[k]
    note = jnp.zeros((ROWS, LANES), F32)
    steps = []
    for number, members in enumerate(pieces_of(len(body), lead_tiles)):
        top, bottom = body[members[0]], body[members[0]]
        for k in members[1:]:
            top, bottom = jnp.maximum(top, body[k]), jnp.minimum(bottom, body[k])
        top = jnp.max(top, axis=1, keepdims=True)
        bottom = jnp.min(bottom, axis=1, keepdims=True)
        middle = 0.5 * top + 0.5 * bottom
        half = jnp.maximum(0.5 * top - 0.5 * bottom, 1e-30)
        note = jnp.where(lane == 2 * number, middle, note)
        note = jnp.where(lane == 2 * number + 1, half * (1.0 / LARGEST), note)
        per_step = jnp.broadcast_to(LARGEST / half, (ROWS, LANES))
        middle = jnp.broadcast_to(middle, (ROWS, LANES))
        steps.extend(jnp.floor((body[k] - middle) * per_step + 0.5) for k in members)
    notes[:, tile(lead_tiles)] = note
    if len(steps) % 2:
        steps.append(jnp.zeros((ROWS, LANES), F32))
    for k in range(len(steps) // 2):
        pair = jnp.concatenate([steps[2 * k], steps[2 * k + 1]], axis=0)
        words[:, tile(k)] = pair.astype(jnp.int32).astype(jnp.int16)


def decode(words, notes, count, lead_tiles):
    tiles = [notes[:, tile(k)] for k in range(lead_tiles)]
    note = notes[:, tile(lead_tiles)]
    steps = []
    for k in range(words.shape[1] // LANES):
        pair = words[:, tile(k)].astype(jnp.int32).astype(F32)
        steps += [pair[:ROWS], pair[ROWS:]]
    for number, members in enumerate(pieces_of(count - lead_tiles, lead_tiles)):
        middle = jnp.broadcast_to(note[:, 2 * number : 2 * number + 1], (ROWS, LANES))
        size = jnp.broadcast_to(note[:, 2 * number + 1 : 2 * number + 2], (ROWS, LANES))
        tiles.extend(steps[k] * size + middle for k in members)
    return tiles


def ordered(mine, theirs, is_upper):
    leading = [jnp.where(is_upper, y, x) for x, y in zip(mine, theirs)]
    trailing = [jnp.where(is_upper, x, y) for x, y in zip(mine, theirs)]
    return leading, trailing


def tiles_of(ref):
    return [ref[:, tile(k)] for k in range(ref.shape[1] // LANES)]


def merge_kernel(level, lead_tiles, info, own, words, notes, other, across, shifts, out, *sent):
    mine = tiles_of(own)
    theirs = decode(words, notes, len(mine), lead_tiles)
    if level == 0:
        for k in range(lead_tiles):
            mine[k], theirs[k] = mine[k] + other[:, tile(k)], theirs[k] + across[:, tile(k)]
    tiles = merged(*ordered(mine, theirs, info[2 + level] == 1), shifts[level], lead_tiles)
    for k, x in enumerate(tiles):
        out[:, tile(k)] = x
    if sent:
        encode(tiles, lead_tiles, *sent)


def back_kernel(level, sizes, info, own, words, notes, shifts, weights, spread, dedispersed, scores, steps):
    frames, lead, tail, factor, window_count, stations = sizes
    first, last = info[0] == 0, info[1] == 1
    lead_tiles, main_tiles, tail_tiles = lead // LANES, frames // LANES, tail // LANES
    if level is None:
        series = tiles_of(own)
    else:
        is_upper = info[2 + level] == 1
        mine = tiles_of(own)
        theirs = decode(words, notes, len(mine), lead_tiles)
        series = merged(*ordered(mine, theirs, is_upper), shifts[level], lead_tiles)
    means = [series[k] * (1.0 / window_count) for k in range(lead_tiles)]
    settled = jnp.broadcast_to(means[-1][:, LANES - 1 :], (ROWS, LANES))
    for k in range(main_tiles + tail_tiles):
        mean = jnp.where(first, means[k], settled) if k < lead_tiles else settled
        value = (series[2 * lead_tiles + k] - mean) * factor
        if k < main_tiles:
            dedispersed[:, tile(k)] = value
        else:
            value = jnp.where(last, 0.0, value)
        steps[k * ROWS : (k + 1) * ROWS, :] = value

    reach = tail_tiles + 1
    parts = []
    for q in range(reach):
        parts.append(
            jnp.concatenate([steps[pl.ds(d + ROWS * q, main_tiles, stride=ROWS), :] for d in range(ROWS)], axis=0)
        )
    operand = jnp.concatenate(parts, axis=1)
    high, low = split(operand)
    weight_high, weight_low = split(weights[...])
    product = lax.dot_general(
        jnp.concatenate([weight_high, weight_high, weight_low], axis=1),
        jnp.concatenate([high, low, high], axis=1),
        NT,
        preferred_element_type=F32,
    )
    blocks = LANES // STRIDE
    templates = product.shape[0] // blocks
    sets = product.shape[1] // LANES
    grouped = jnp.concatenate(
        [
            jnp.concatenate([product[i * templates : (i + 1) * templates, tile(a)] for i in range(blocks)], axis=1)
            for a in range(sets)
        ],
        axis=0,
    )
    one = grouped.astype(BF)
    rest = grouped - one.astype(F32)
    two = rest.astype(BF)
    three = (rest - two.astype(F32)).astype(BF)
    placed = jnp.dot(jnp.concatenate([one, two, three], axis=0), spread[...], preferred_element_type=F32)
    count = sets * templates
    placed = placed[:count] + placed[count : 2 * count] + placed[2 * count :]
    trials = LANES // main_tiles
    positions = main_tiles * blocks
    for a in range(sets):
        for d in range(trials):
            scores[a * trials + d] = placed[a * templates : (a + 1) * templates, d * positions : (d + 1) * positions]


def swapped(x, axis, distance):
    return lax.ppermute(x, axis, [(i, i ^ distance) for i in range(lax.axis_size(axis))])


def template_weights(tap_index, tap_weight, reach):
    hit = tap_index[:, :, None] == jnp.arange(WIN, dtype=jnp.int32)[None, None, :]
    template = jnp.sum(jnp.where(hit, tap_weight[:, :, None], 0.0), axis=1)
    width = reach * LANES
    rows = [
        jnp.pad(template, ((0, 0), (i * STRIDE, width - WIN - i * STRIDE))) for i in range(LANES // STRIDE)
    ]
    return jnp.concatenate(rows, axis=0)


def wide_merge(own, partner, is_upper, shifts):
    leading = jnp.where(is_upper, partner, own)
    trailing = jnp.where(is_upper, own, partner)
    place = jnp.arange(own.shape[1], dtype=jnp.int32)[None, :] - shifts[:, None]
    picked = jnp.take_along_axis(trailing, jnp.maximum(place, 0), axis=1)
    return leading + jnp.where(place >= 0, picked, 0.0)


def on_device(voltages, pfb_taps, local_shift, cross_shift, tap_index, tap_weight):
    frames, channels = voltages.shape[1:]
    tap_count = pfb_taps.shape[0]
    trials = cross_shift.shape[1]
    local_levels = local_shift.shape[0]
    tm_size, freq_size = lax.axis_size("tm"), lax.axis_size("freq")
    levels = freq_size.bit_length() - 1
    group = channels // trials
    margin = round_up(tap_count, 16)
    cross_reach = sum(trials * 2**level - 1 for level in range(levels))
    lead = round_up(local_levels * (LSHIFT - 1) + cross_reach, LANES)
    tail = round_up(WIN - STRIDE, LANES)

    time, freq = lax.axis_index("tm"), lax.axis_index("freq")
    info = jnp.stack(
        [time, (time == tm_size - 1).astype(jnp.int32)] + [freq >> level & 1 for level in range(max(levels, 1))]
    ).astype(jnp.int32)
    halo_rows = round_up(max(lead + margin, tail), 16)
    if tm_size == 2:
        start = jnp.where(time == 0, frames - halo_rows, 0)
        sent = lax.dynamic_slice_in_dim(voltages, start, halo_rows, axis=1)
        halo = swapped(sent, "tm", 1)
    else:
        raise NotImplementedError("tm")

    chunk_tiles, pieces = 12, 4
    table = jnp.asarray(dft_table(channels, group))
    extended = lead + frames + tail
    width = lead + extended

    sizes = (frames, lead, tail, chunk_tiles, pieces, tap_count) + local_shift.shape
    wide = 2 * channels
    spare = ((0, -(tap_count + local_levels) % ROWS), (0, wide - local_shift.shape[1]))
    packed = jnp.concatenate(
        [table, jnp.pad(pfb_taps, ((0, 0), (0, wide - channels))), jnp.pad(local_shift.astype(F32), spare)], axis=0
    )

    def front(*refs):
        front_kernel(sizes, *refs)

    lead_tiles, body_tiles = lead // LANES, extended // LANES
    sent_shapes = (
        jax.ShapeDtypeStruct((2 * ROWS, -(-body_tiles // 2) * LANES), jnp.int16),
        jax.ShapeDtypeStruct((trials, lead + LANES), F32),
    )
    series_shape = jax.ShapeDtypeStruct((trials, width), F32)
    series, *sent = pl.pallas_call(
        front,
        out_shape=(series_shape,) + sent_shapes,
        in_specs=[SMEM, ANY, VMEM, VMEM],
        out_specs=(VMEM,) * 3,
        scratch_shapes=[
            pltpu.VMEM(voltages.shape, BF),
            pltpu.VMEM((2, margin + extended, channels), F32),
            *[pltpu.VMEM((chunk_tiles * LANES, channels), F32)] * 4,
            *[pltpu.VMEM((chunk_tiles * LANES, 2 * channels), F32)] * 2,
            pltpu.VMEM((trials, width), F32),
            pltpu.VMEM((channels, LANES), F32),
            pltpu.SemaphoreType.DMA((pieces,)),
        ],
        compiler_params=pltpu.CompilerParams(vmem_limit_bytes=52 * 1024 * 1024),
        cost_estimate=pl.CostEstimate(flops=2 * 10**10, bytes_accessed=4096, transcendentals=0),
        name="front",
    )(info, voltages, halo, packed)

    shift_rows = jnp.broadcast_to(cross_shift[:, :, None], cross_shift.shape + (LANES,))
    short = [level for level in range(levels) if trials * 2**level <= LANES]
    fused = len(short) == levels > 1
    response = sent[1][:, :lead]
    other = swapped(response, "tm", 1)
    for level in range(levels - 1 if fused else levels):
        if level in short:
            if level == min(1, levels - 2):
                (tap_index, tap_weight), sent = lax.optimization_barrier(((tap_index, tap_weight), sent))
                weights = template_weights(tap_index, tap_weight, tail // LANES + 1)
            received = [swapped(x, "freq", 2**level) for x in sent]
            if level == min(1, levels - 2):
                received[0], weights = lax.optimization_barrier((received[0], weights))
            if level == 0:
                pairs = [(i, i ^ tm_size ^ 1) for i in range(freq_size * tm_size)]
                across = lax.ppermute(response, ("freq", "tm"), pairs)
            shapes = (series_shape,) + (sent_shapes if level + 1 in short else ())

            def merge(*refs, level=level):
                merge_kernel(level, lead_tiles, *refs)

            series, *sent = pl.pallas_call(
                merge,
                out_shape=shapes,
                in_specs=[SMEM] + [VMEM] * 6,
                out_specs=(VMEM,) * len(shapes),
                compiler_params=PARAMS,
                name="merge",
            )(info, series, *received, other, across, shift_rows)
        else:
            partner = swapped(series, "freq", 2**level)
            series = wide_merge(series, partner, info[2 + level] == 1, cross_shift[level])

    if fused:
        last_level = levels - 1
        received = [swapped(x, "freq", 2**last_level) for x in sent]
    else:
        last_level = None
        received = [other, other]

    templates = tap_index.shape[0]
    spread = jnp.asarray(spread_table(frames // LANES, LANES // STRIDE))
    factor = 1.0 / (channels * math.sqrt(channels * freq_size))

    def back(*refs):
        back_kernel(last_level, (frames, lead, tail, factor, frames * tm_size, STRIDE), *refs)

    return pl.pallas_call(
        back,
        out_shape=(
            jax.ShapeDtypeStruct((trials, frames), F32),
            jax.ShapeDtypeStruct((trials, templates, frames // STRIDE), F32),
        ),
        in_specs=[SMEM] + [VMEM] * 6,
        out_specs=(VMEM, VMEM),
        scratch_shapes=[pltpu.VMEM(((frames + tail) // LANES * ROWS, LANES), F32)],
        compiler_params=PARAMS,
        name="back",
    )(info, series, *received, shift_rows, weights, spread)


def solution(mesh):
    return jax.shard_map(
        on_device,
        mesh=mesh,
        in_specs=(P("beam", "tm", "freq"), P(), P(None, "freq"), P(None, "freq"), P(), P()),
        out_specs=(P(("beam", "freq"), "tm"), P(("beam", "freq"), None, "tm")),
        check_vma=False,
    )
```

```python
import math

import jax
import jax.numpy as jnp
import numpy as np
from jax import lax
from jax.experimental import pallas as pl
from jax.experimental.pallas import tpu as pltpu
from jax.sharding import PartitionSpec as P

LSHIFT = 8
STRIDE = 32
WIN = 256
SET = 5
LARGEST = 32000.0
LANES = 128
ROWS = 8
BF = jnp.bfloat16
F32 = jnp.float32
NT = (((1,), (1,)), ((), ()))
VMEM = pl.BlockSpec(memory_space=pltpu.VMEM)
SMEM = pl.BlockSpec(memory_space=pltpu.SMEM)
ANY = pl.BlockSpec(memory_space=pl.ANY)
PARAMS = pltpu.CompilerParams(vmem_limit_bytes=48 * 1024 * 1024)


def round_up(value, multiple):
    return -(-value // multiple) * multiple


def whole(array):
    return pl.BlockSpec(array.shape, lambda *_: (0,) * array.ndim)


def tile(k):
    return slice(k * LANES, (k + 1) * LANES)


def split(x):
    high = x.astype(BF)
    return high, (x - high.astype(F32)).astype(BF)


def lanes():
    return lax.broadcasted_iota(jnp.int32, (ROWS, LANES), 1)


def rotated(x, index):
    return jnp.take_along_axis(x, index, axis=1, mode="promise_in_bounds")


def merged(leading, trailing, shifts, lead_tiles):
    lane = lanes()
    index = (lane - shifts) & (LANES - 1)
    inside = lane >= shifts
    out = []
    for k, (lead, trail) in enumerate(zip(leading, trailing)):
        if k in (0, lead_tiles):
            before = jnp.zeros((ROWS, LANES), F32)
        turned = rotated(trail, index)
        out.append(lead + jnp.where(inside, turned, before))
        before = turned
    return out


def dft_table(channels, group):
    place = np.arange(channels)
    number = (place % (channels // group)) * group + place // (channels // group)
    phase = (np.arange(channels)[:, None] * number[None, :]) % channels
    angle = phase * (2.0 * np.pi / channels)
    cosine, sine = np.cos(angle), np.sin(angle)
    return np.block([[cosine, -sine], [sine, cosine]]).T.astype(np.float32)


def spread_table(tiles, blocks):
    trials = LANES // tiles
    table = np.zeros((blocks, trials, tiles, trials, tiles * blocks), np.float32)
    for block in range(blocks):
        for trial in range(trials):
            for number in range(tiles):
                table[block, trial, number, trial, number * blocks + block] = 1.0
    return table.reshape(blocks * LANES, -1).astype(jnp.bfloat16)


def front_kernel(
    sizes, info, volts, beside, packed, out, words, notes, held, samples, *scratch
):
    filtered, spectra = (scratch[:2], scratch[2:4]), scratch[4:6]
    series, sums, arrived = scratch[6:]
    frames, lead, tail, chunk_tiles, pieces, tap_count, level_count, columns = sizes
    channels = volts.shape[2]
    taps_at, shifts_at = 2 * channels, 2 * channels + tap_count
    group_count = channels // ROWS
    margin = round_up(tap_count, 16)
    halo_rows = beside.shape[1]
    first, last = info[0] == 0, info[1] == 1
    piece = frames // pieces

    def copies(number):
        rows = slice(number * piece, (number + 1) * piece)
        return pltpu.make_async_copy(volts.at[:, rows, :], held.at[:, rows, :], arrived.at[number])

    copies(0).start()
    for number in range(1, pieces):
        copies(number).start()

    place = lax.broadcasted_iota(jnp.int32, (channels, columns), 0)
    column = lax.broadcasted_iota(jnp.int32, (channels, columns), 1)
    channel = (place & (ROWS - 1)) * group_count + (place >> (ROWS.bit_length() - 1))
    single_levels = group_count.bit_length() - 1

    def picked(hit, level):
        row = jnp.broadcast_to(packed[shifts_at + level : shifts_at + level + 1, :columns], (LANES, columns))
        return lax.dot_general(hit.astype(F32), row, NT, preferred_element_type=F32)

    total = jnp.zeros((channels, LANES), F32)
    for level in range(single_levels):
        trailing = (channel >> level & 1) == 1
        spot = (channel >> (level + 1)) << level
        total = total + picked(jnp.logical_and(trailing, column == spot), level)
    total = total.astype(jnp.int32)
    shift = [total[j * ROWS : (j + 1) * ROWS] for j in range(group_count)]
    lane = lanes()
    lead_tiles, main_tiles, tail_tiles = lead // LANES, frames // LANES, tail // LANES
    tile_count = lead_tiles + main_tiles + tail_tiles

    def convert(number):
        if number == pieces:
            for part in range(2):
                before = beside[part, halo_rows - lead - margin :, :].astype(F32)
                samples[part, : lead + margin, :] = jnp.where(first, 0.0, before)
                after = beside[part, :tail, :].astype(F32)
                samples[part, lead + margin + frames :, :] = jnp.where(last, 0.0, after)
            return
        copies(number).wait()
        rows = slice(number * piece, (number + 1) * piece)
        at = lead + margin + number * piece
        for part in range(2):
            samples[part, at : at + piece, :] = held[part, rows, :].astype(F32)

    def filter_tile(number, into):
        for part in range(2):
            base = number * LANES + margin
            value = samples[part, base : base + LANES, :] * packed[taps_at : taps_at + 1, :channels]
            for k in range(1, tap_count):
                value = value + samples[part, base - k : base - k + LANES, :] * packed[taps_at + k : taps_at + k + 1, :channels]
            filtered[into[0]][part][into[1] * LANES : (into[1] + 1) * LANES, :] = value

    def transform(slot, count):
        rows = slice(0, count * LANES)
        both = jnp.concatenate([filtered[slot][0][rows, :], filtered[slot][1][rows, :]], axis=1)
        spectra[slot][:, rows] = lax.dot_general(
            packed[:taps_at, :], both, NT, preferred_element_type=F32, precision=lax.Precision.HIGH
        )

    def collapse_tile(number, slot, sub, earlier):
        real, imag = spectra[slot][:channels, tile(sub)], spectra[slot][channels:, tile(sub)]
        power = real * real + imag * imag
        counted = lead_tiles <= number < lead_tiles + main_tiles
        acc = jnp.zeros((ROWS, LANES), F32)
        now = []
        for j in range(group_count):
            rows = slice(j * ROWS, (j + 1) * ROWS)
            value = power[rows]
            turned = rotated(value, (lane - shift[j]) & (LANES - 1))
            acc = acc + jnp.where(lane >= shift[j], turned, earlier[j])
            now.append(turned)
            if counted:
                sums[rows] += value
        series[:, tile(lead_tiles + number)] = acc
        return now

    sums[...] = jnp.zeros_like(sums)
    starts = list(range(0, tile_count, chunk_tiles)) + [tile_count]
    chunks = len(starts) - 1
    earlier = [jnp.zeros((ROWS, LANES), F32)] * group_count
    converted = 0
    convert(pieces)
    for step in range(chunks + 2):
        if step < chunks:
            needed = min(pieces, -(-((starts[step + 1] - lead_tiles) * LANES) // piece))
            while converted < needed:
                convert(converted)
                converted += 1
        if 1 <= step <= chunks:
            transform((step - 1) % 2, starts[step] - starts[step - 1])
        for sub in range(chunk_tiles):
            if step < chunks and starts[step] + sub < starts[step + 1]:
                filter_tile(starts[step] + sub, (step % 2, sub))
            if step >= 2 and starts[step - 2] + sub < starts[step - 1]:
                earlier = collapse_tile(starts[step - 2] + sub, step % 2, sub, earlier)

    settled = jnp.zeros((ROWS, LANES), F32)
    begun = jnp.zeros((ROWS, LANES), F32)
    for j in range(group_count):
        rows = slice(j * ROWS, (j + 1) * ROWS)
        channel_sum = jnp.broadcast_to(jnp.sum(sums[rows], axis=1, keepdims=True), (ROWS, LANES))
        settled = settled + channel_sum
        begun = begun + jnp.where(lane >= shift[j], channel_sum, 0.0)
    series[:, :LANES] = begun
    for k in range(1, lead_tiles):
        series[:, tile(k)] = settled

    tiles = [series[:, tile(k)] for k in range(lead_tiles + tile_count)]
    row = lax.broadcasted_iota(jnp.int32, (ROWS, LANES), 0)
    slot_row = lax.broadcasted_iota(jnp.int32, (ROWS, columns), 0)
    slot_column = lax.broadcasted_iota(jnp.int32, (ROWS, columns), 1)
    for step in range(level_count - single_levels):
        level = single_levels + step
        distance = 2**step
        upper = (row & distance) > 0
        leading = [jnp.where(upper, pltpu.roll(x, distance, 0), x) for x in tiles]
        trailing = [jnp.where(upper, x, pltpu.roll(x, ROWS - distance, 0)) for x in tiles]
        spot = ((slot_row >> (step + 1)) << level) + (slot_row & (2 * distance - 1))
        tiles = merged(leading, trailing, picked(slot_column == spot, level).astype(jnp.int32), lead_tiles)
    for k, x in enumerate(tiles):
        out[:, tile(k)] = x
    encode(tiles, lead_tiles, words, notes)


def pieces_of(count, lead_tiles):
    starts = [0] + list(range(lead_tiles, count, SET)) + [count]
    return [range(at, to) for at, to in zip(starts[:-1], starts[1:])]


def encode(tiles, lead_tiles, words, notes):
    lane = lanes()
    body = tiles[lead_tiles:]
    for k in range(lead_tiles):
        notes[:, tile(k)] = tiles[k]
    note = jnp.zeros((ROWS, LANES), F32)
    steps = []
    for number, members in enumerate(pieces_of(len(body), lead_tiles)):
        top, bottom = body[members[0]], body[members[0]]
        for k in members[1:]:
            top, bottom = jnp.maximum(top, body[k]), jnp.minimum(bottom, body[k])
        top = jnp.max(top, axis=1, keepdims=True)
        bottom = jnp.min(bottom, axis=1, keepdims=True)
        middle = 0.5 * top + 0.5 * bottom
        half = jnp.maximum(0.5 * top - 0.5 * bottom, 1e-30)
        note = jnp.where(lane == 2 * number, middle, note)
        note = jnp.where(lane == 2 * number + 1, half * (1.0 / LARGEST), note)
        per_step = jnp.broadcast_to(LARGEST / half, (ROWS, LANES))
        middle = jnp.broadcast_to(middle, (ROWS, LANES))
        steps.extend(jnp.floor((body[k] - middle) * per_step + 0.5) for k in members)
    notes[:, tile(lead_tiles)] = note
    if len(steps) % 2:
        steps.append(jnp.zeros((ROWS, LANES), F32))
    for k in range(len(steps) // 2):
        pair = jnp.concatenate([steps[2 * k], steps[2 * k + 1]], axis=0)
        words[:, tile(k)] = pair.astype(jnp.int32).astype(jnp.int16)


def decode(words, notes, count, lead_tiles):
    tiles = [notes[:, tile(k)] for k in range(lead_tiles)]
    note = notes[:, tile(lead_tiles)]
    steps = []
    for k in range(words.shape[1] // LANES):
        pair = words[:, tile(k)].astype(jnp.int32).astype(F32)
        steps += [pair[:ROWS], pair[ROWS:]]
    for number, members in enumerate(pieces_of(count - lead_tiles, lead_tiles)):
        middle = jnp.broadcast_to(note[:, 2 * number : 2 * number + 1], (ROWS, LANES))
        size = jnp.broadcast_to(note[:, 2 * number + 1 : 2 * number + 2], (ROWS, LANES))
        tiles.extend(steps[k] * size + middle for k in members)
    return tiles


def ordered(mine, theirs, is_upper):
    leading = [jnp.where(is_upper, y, x) for x, y in zip(mine, theirs)]
    trailing = [jnp.where(is_upper, x, y) for x, y in zip(mine, theirs)]
    return leading, trailing


def tiles_of(ref):
    return [ref[:, tile(k)] for k in range(ref.shape[1] // LANES)]


def merge_kernel(level, lead_tiles, info, own, words, notes, other, across, shifts, out, *sent):
    mine = tiles_of(own)
    theirs = decode(words, notes, len(mine), lead_tiles)
    if level == 0:
        for k in range(lead_tiles):
            mine[k], theirs[k] = mine[k] + other[:, tile(k)], theirs[k] + across[:, tile(k)]
    tiles = merged(*ordered(mine, theirs, info[2 + level] == 1), shifts[level], lead_tiles)
    for k, x in enumerate(tiles):
        out[:, tile(k)] = x
    if sent:
        encode(tiles, lead_tiles, *sent)


def back_kernel(level, sizes, info, own, words, notes, shifts, weights, spread, dedispersed, scores, steps):
    frames, lead, tail, factor, window_count, stations = sizes
    first, last = info[0] == 0, info[1] == 1
    lead_tiles, main_tiles, tail_tiles = lead // LANES, frames // LANES, tail // LANES
    if level is None:
        series = tiles_of(own)
    else:
        is_upper = info[2 + level] == 1
        mine = tiles_of(own)
        theirs = decode(words, notes, len(mine), lead_tiles)
        series = merged(*ordered(mine, theirs, is_upper), shifts[level], lead_tiles)
    means = [series[k] * (1.0 / window_count) for k in range(lead_tiles)]
    settled = jnp.broadcast_to(means[-1][:, LANES - 1 :], (ROWS, LANES))
    for k in range(main_tiles + tail_tiles):
        mean = jnp.where(first, means[k], settled) if k < lead_tiles else settled
        value = (series[2 * lead_tiles + k] - mean) * factor
        if k < main_tiles:
            dedispersed[:, tile(k)] = value
        else:
            value = jnp.where(last, 0.0, value)
        steps[k * ROWS : (k + 1) * ROWS, :] = value

    reach = tail_tiles + 1
    parts = []
    for q in range(reach):
        parts.append(
            jnp.concatenate([steps[pl.ds(d + ROWS * q, main_tiles, stride=ROWS), :] for d in range(ROWS)], axis=0)
        )
    operand = jnp.concatenate(parts, axis=1)
    high, low = split(operand)
    weight_high, weight_low = split(weights[...])
    product = lax.dot_general(
        jnp.concatenate([weight_high, weight_high, weight_low], axis=1),
        jnp.concatenate([high, low, high], axis=1),
        NT,
        preferred_element_type=F32,
    )
    blocks = LANES // STRIDE
    templates = product.shape[0] // blocks
    sets = product.shape[1] // LANES
    grouped = jnp.concatenate(
        [
            jnp.concatenate([product[i * templates : (i + 1) * templates, tile(a)] for i in range(blocks)], axis=1)
            for a in range(sets)
        ],
        axis=0,
    )
    placed = jnp.dot(jnp.concatenate(split(grouped), axis=0), spread[...], preferred_element_type=F32)
    count = sets * templates
    placed = placed[:count] + placed[count:]
    trials = LANES // main_tiles
    positions = main_tiles * blocks
    for a in range(sets):
        for d in range(trials):
            scores[a * trials + d] = placed[a * templates : (a + 1) * templates, d * positions : (d + 1) * positions]


def swapped(x, axis, distance):
    return lax.ppermute(x, axis, [(i, i ^ distance) for i in range(lax.axis_size(axis))])


def template_weights(tap_index, tap_weight, reach):
    hit = tap_index[:, :, None] == jnp.arange(WIN, dtype=jnp.int32)[None, None, :]
    template = jnp.sum(jnp.where(hit, tap_weight[:, :, None], 0.0), axis=1)
    width = reach * LANES
    rows = [
        jnp.pad(template, ((0, 0), (i * STRIDE, width - WIN - i * STRIDE))) for i in range(LANES // STRIDE)
    ]
    return jnp.concatenate(rows, axis=0)


def wide_merge(own, partner, is_upper, shifts):
    leading = jnp.where(is_upper, partner, own)
    trailing = jnp.where(is_upper, own, partner)
    place = jnp.arange(own.shape[1], dtype=jnp.int32)[None, :] - shifts[:, None]
    picked = jnp.take_along_axis(trailing, jnp.maximum(place, 0), axis=1)
    return leading + jnp.where(place >= 0, picked, 0.0)


def on_device(voltages, pfb_taps, local_shift, cross_shift, tap_index, tap_weight):
    frames, channels = voltages.shape[1:]
    tap_count = pfb_taps.shape[0]
    trials = cross_shift.shape[1]
    local_levels = local_shift.shape[0]
    tm_size, freq_size = lax.axis_size("tm"), lax.axis_size("freq")
    levels = freq_size.bit_length() - 1
    group = channels // trials
    margin = round_up(tap_count, 16)
    cross_reach = sum(trials * 2**level - 1 for level in range(levels))
    lead = round_up(local_levels * (LSHIFT - 1) + cross_reach, LANES)
    tail = round_up(WIN - STRIDE, LANES)

    time, freq = lax.axis_index("tm"), lax.axis_index("freq")
    info = jnp.stack(
        [time, (time == tm_size - 1).astype(jnp.int32)] + [freq >> level & 1 for level in range(max(levels, 1))]
    ).astype(jnp.int32)
    halo_rows = round_up(max(lead + margin, tail), 16)
    if tm_size == 2:
        start = jnp.where(time == 0, frames - halo_rows, 0)
        sent = lax.dynamic_slice_in_dim(voltages, start, halo_rows, axis=1)
        halo = swapped(sent, "tm", 1)
    else:
        raise NotImplementedError("tm")

    chunk_tiles, pieces = 12, 4
    table = jnp.asarray(dft_table(channels, group))
    extended = lead + frames + tail
    width = lead + extended

    sizes = (frames, lead, tail, chunk_tiles, pieces, tap_count) + local_shift.shape
    wide = 2 * channels
    spare = ((0, -(tap_count + local_levels) % ROWS), (0, wide - local_shift.shape[1]))
    packed = jnp.concatenate(
        [table, jnp.pad(pfb_taps, ((0, 0), (0, wide - channels))), jnp.pad(local_shift, spare).astype(F32)], axis=0
    )

    def front(*refs):
        front_kernel(sizes, *refs)

    lead_tiles, body_tiles = lead // LANES, extended // LANES
    sent_shapes = (
        jax.ShapeDtypeStruct((2 * ROWS, -(-body_tiles // 2) * LANES), jnp.int16),
        jax.ShapeDtypeStruct((trials, lead + LANES), F32),
    )
    series_shape = jax.ShapeDtypeStruct((trials, width), F32)
    series, *sent = pl.pallas_call(
        front,
        out_shape=(series_shape,) + sent_shapes,
        in_specs=[SMEM, ANY, VMEM, VMEM],
        out_specs=(VMEM,) * 3,
        scratch_shapes=[
            pltpu.VMEM(voltages.shape, BF),
            pltpu.VMEM((2, margin + extended, channels), F32),
            *[pltpu.VMEM((chunk_tiles * LANES, channels), F32)] * 4,
            *[pltpu.VMEM((2 * channels, chunk_tiles * LANES), F32)] * 2,
            pltpu.VMEM((trials, width), F32),
            pltpu.VMEM((channels, LANES), F32),
            pltpu.SemaphoreType.DMA((pieces,)),
        ],
        compiler_params=pltpu.CompilerParams(vmem_limit_bytes=52 * 1024 * 1024),
        cost_estimate=pl.CostEstimate(flops=2 * 10**10, bytes_accessed=4096, transcendentals=0),
        name="front",
    )(info, voltages, halo, packed)

    shift_rows = jnp.broadcast_to(cross_shift[:, :, None], cross_shift.shape + (LANES,))
    short = [level for level in range(levels) if trials * 2**level <= LANES]
    fused = len(short) == levels > 1
    response = sent[1][:, :lead]
    other = swapped(response, "tm", 1)
    for level in range(levels - 1 if fused else levels):
        if level in short:
            if level == min(1, levels - 2):
                (tap_index, tap_weight), sent = lax.optimization_barrier(((tap_index, tap_weight), sent))
                weights = template_weights(tap_index, tap_weight, tail // LANES + 1)
            received = [swapped(x, "freq", 2**level) for x in sent]
            if level == min(1, levels - 2):
                received[0], weights = lax.optimization_barrier((received[0], weights))
            if level == 0:
                pairs = [(i, i ^ tm_size ^ 1) for i in range(freq_size * tm_size)]
                across = lax.ppermute(response, ("freq", "tm"), pairs)
            shapes = (series_shape,) + (sent_shapes if level + 1 in short else ())

            def merge(*refs, level=level):
                merge_kernel(level, lead_tiles, *refs)

            series, *sent = pl.pallas_call(
                merge,
                out_shape=shapes,
                in_specs=[SMEM] + [VMEM] * 6,
                out_specs=(VMEM,) * len(shapes),
                compiler_params=PARAMS,
                name="merge",
            )(info, series, *received, other, across, shift_rows)
        else:
            partner = swapped(series, "freq", 2**level)
            series = wide_merge(series, partner, info[2 + level] == 1, cross_shift[level])

    if fused:
        last_level = levels - 1
        received = [swapped(x, "freq", 2**last_level) for x in sent]
    else:
        last_level = None
        received = [other, other]

    templates = tap_index.shape[0]
    spread = jnp.asarray(spread_table(frames // LANES, LANES // STRIDE))
    factor = 1.0 / (channels * math.sqrt(channels * freq_size))

    def back(*refs):
        back_kernel(last_level, (frames, lead, tail, factor, frames * tm_size, STRIDE), *refs)

    return pl.pallas_call(
        back,
        out_shape=(
            jax.ShapeDtypeStruct((trials, frames), F32),
            jax.ShapeDtypeStruct((trials, templates, frames // STRIDE), F32),
        ),
        in_specs=[SMEM] + [VMEM] * 6,
        out_specs=(VMEM, VMEM),
        scratch_shapes=[pltpu.VMEM(((frames + tail) // LANES * ROWS + ROWS, LANES), F32)],
        compiler_params=PARAMS,
        name="back",
    )(info, series, *received, shift_rows, weights, spread)


def solution(mesh):
    return jax.shard_map(
        on_device,
        mesh=mesh,
        in_specs=(P("beam", "tm", "freq"), P(), P(None, "freq"), P(None, "freq"), P(), P()),
        out_specs=(P(("beam", "freq"), "tm"), P(("beam", "freq"), None, "tm")),
        check_vma=False,
    )
```

```python
import math

import jax
import jax.numpy as jnp
import numpy as np
from jax import lax
from jax.experimental import pallas as pl
from jax.experimental.pallas import tpu as pltpu
from jax.sharding import PartitionSpec as P

LSHIFT = 8
STRIDE = 32
WIN = 256
SET = 5
LARGEST = 32000.0
LANES = 128
ROWS = 8
BF = jnp.bfloat16
F32 = jnp.float32
NT = (((1,), (1,)), ((), ()))
VMEM = pl.BlockSpec(memory_space=pltpu.VMEM)
SMEM = pl.BlockSpec(memory_space=pltpu.SMEM)
ANY = pl.BlockSpec(memory_space=pl.ANY)
PARAMS = pltpu.CompilerParams(vmem_limit_bytes=48 * 1024 * 1024)


def round_up(value, multiple):
    return -(-value // multiple) * multiple


def whole(array):
    return pl.BlockSpec(array.shape, lambda *_: (0,) * array.ndim)


def tile(k):
    return slice(k * LANES, (k + 1) * LANES)


def split(x):
    high = x.astype(BF)
    return high, (x - high.astype(F32)).astype(BF)


def lanes():
    return lax.broadcasted_iota(jnp.int32, (ROWS, LANES), 1)


def rotated(x, index):
    return jnp.take_along_axis(x, index, axis=1, mode="promise_in_bounds")


def merged(leading, trailing, shifts, lead_tiles):
    lane = lanes()
    index = (lane - shifts) & (LANES - 1)
    inside = lane >= shifts
    out = []
    for k, (lead, trail) in enumerate(zip(leading, trailing)):
        if k in (0, lead_tiles):
            before = jnp.zeros((ROWS, LANES), F32)
        turned = rotated(trail, index)
        out.append(lead + jnp.where(inside, turned, before))
        before = turned
    return out


def dft_table(channels, group):
    place = np.arange(channels)
    number = (place % (channels // group)) * group + place // (channels // group)
    phase = (np.arange(channels)[:, None] * number[None, :]) % channels
    angle = phase * (2.0 * np.pi / channels)
    cosine, sine = np.cos(angle), np.sin(angle)
    return np.block([[cosine, -sine], [sine, cosine]]).T.astype(np.float32)


def spread_table(tiles, blocks):
    trials = LANES // tiles
    table = np.zeros((blocks, trials, tiles, trials, tiles * blocks), np.float32)
    for block in range(blocks):
        for trial in range(trials):
            for number in range(tiles):
                table[block, trial, number, trial, number * blocks + block] = 1.0
    return table.reshape(blocks * LANES, -1).astype(jnp.bfloat16)


def front_kernel(
    sizes, info, volts, beside, packed, shifts, out, words, notes, held, samples, *scratch
):
    filtered, spectra = (scratch[:2], scratch[2:4]), scratch[4:6]
    series, sums, arrived = scratch[6:]
    frames, lead, tail, chunk_tiles, pieces, tap_count, level_count, columns = sizes
    channels = volts.shape[2]
    taps_at = 2 * channels
    group_count = channels // ROWS
    margin = round_up(tap_count, 16)
    halo_rows = beside.shape[1]
    first, last = info[0] == 0, info[1] == 1
    piece = frames // pieces

    def copies(number):
        rows = slice(number * piece, (number + 1) * piece)
        return pltpu.make_async_copy(volts.at[:, rows, :], held.at[:, rows, :], arrived.at[number])

    copies(0).start()
    for number in range(1, pieces):
        copies(number).start()

    place = lax.broadcasted_iota(jnp.int32, (channels, columns), 0)
    column = lax.broadcasted_iota(jnp.int32, (channels, columns), 1)
    channel = (place & (ROWS - 1)) * group_count + (place >> (ROWS.bit_length() - 1))
    single_levels = group_count.bit_length() - 1

    def picked(hit, level):
        row = jnp.broadcast_to(shifts[level : level + 1, :].astype(F32), (LANES, columns))
        return lax.dot_general(hit.astype(F32), row, NT, preferred_element_type=F32)

    total = jnp.zeros((channels, LANES), F32)
    for level in range(single_levels):
        trailing = (channel >> level & 1) == 1
        spot = (channel >> (level + 1)) << level
        total = total + picked(jnp.logical_and(trailing, column == spot), level)
    total = total.astype(jnp.int32)
    shift = [total[j * ROWS : (j + 1) * ROWS] for j in range(group_count)]
    lane = lanes()
    lead_tiles, main_tiles, tail_tiles = lead // LANES, frames // LANES, tail // LANES
    tile_count = lead_tiles + main_tiles + tail_tiles

    def convert(number):
        if number == pieces:
            for part in range(2):
                before = beside[part, halo_rows - lead - margin :, :].astype(F32)
                samples[part, : lead + margin, :] = jnp.where(first, 0.0, before)
                after = beside[part, :tail, :].astype(F32)
                samples[part, lead + margin + frames :, :] = jnp.where(last, 0.0, after)
            return
        copies(number).wait()
        rows = slice(number * piece, (number + 1) * piece)
        at = lead + margin + number * piece
        for part in range(2):
            samples[part, at : at + piece, :] = held[part, rows, :].astype(F32)

    def filter_tile(number, into):
        for part in range(2):
            base = number * LANES + margin
            value = samples[part, base : base + LANES, :] * packed[taps_at : taps_at + 1, :channels]
            for k in range(1, tap_count):
                value = value + samples[part, base - k : base - k + LANES, :] * packed[taps_at + k : taps_at + k + 1, :channels]
            filtered[into[0]][part][into[1] * LANES : (into[1] + 1) * LANES, :] = value

    def transform(slot, count):
        rows = slice(0, count * LANES)
        both = jnp.concatenate([filtered[slot][0][rows, :], filtered[slot][1][rows, :]], axis=1)
        spectra[slot][:, rows] = lax.dot_general(
            packed[:taps_at, :], both, NT, preferred_element_type=F32, precision=lax.Precision.HIGH
        )

    def collapse_tile(number, slot, sub, earlier):
        real, imag = spectra[slot][:channels, tile(sub)], spectra[slot][channels:, tile(sub)]
        power = real * real + imag * imag
        counted = lead_tiles <= number < lead_tiles + main_tiles
        acc = jnp.zeros((ROWS, LANES), F32)
        now = []
        for j in range(group_count):
            rows = slice(j * ROWS, (j + 1) * ROWS)
            value = power[rows]
            turned = rotated(value, (lane - shift[j]) & (LANES - 1))
            acc = acc + jnp.where(lane >= shift[j], turned, earlier[j])
            now.append(turned)
            if counted:
                sums[rows] += value
        series[:, tile(lead_tiles + number)] = acc
        return now

    sums[...] = jnp.zeros_like(sums)
    starts = list(range(0, tile_count, chunk_tiles)) + [tile_count]
    chunks = len(starts) - 1
    earlier = [jnp.zeros((ROWS, LANES), F32)] * group_count
    converted = 0
    convert(pieces)
    for step in range(chunks + 2):
        if step < chunks:
            needed = min(pieces, -(-((starts[step + 1] - lead_tiles) * LANES) // piece))
            while converted < needed:
                convert(converted)
                converted += 1
        if 1 <= step <= chunks:
            transform((step - 1) % 2, starts[step] - starts[step - 1])
        for sub in range(chunk_tiles):
            if step < chunks and starts[step] + sub < starts[step + 1]:
                filter_tile(starts[step] + sub, (step % 2, sub))
            if step >= 2 and starts[step - 2] + sub < starts[step - 1]:
                earlier = collapse_tile(starts[step - 2] + sub, step % 2, sub, earlier)

    settled = jnp.zeros((ROWS, LANES), F32)
    begun = jnp.zeros((ROWS, LANES), F32)
    for j in range(group_count):
        rows = slice(j * ROWS, (j + 1) * ROWS)
        channel_sum = jnp.broadcast_to(jnp.sum(sums[rows], axis=1, keepdims=True), (ROWS, LANES))
        settled = settled + channel_sum
        begun = begun + jnp.where(lane >= shift[j], channel_sum, 0.0)
    series[:, :LANES] = begun
    for k in range(1, lead_tiles):
        series[:, tile(k)] = settled

    tiles = [series[:, tile(k)] for k in range(lead_tiles + tile_count)]
    row = lax.broadcasted_iota(jnp.int32, (ROWS, LANES), 0)
    slot_row = lax.broadcasted_iota(jnp.int32, (ROWS, columns), 0)
    slot_column = lax.broadcasted_iota(jnp.int32, (ROWS, columns), 1)
    for step in range(level_count - single_levels):
        level = single_levels + step
        distance = 2**step
        upper = (row & distance) > 0
        leading = [jnp.where(upper, pltpu.roll(x, distance, 0), x) for x in tiles]
        trailing = [jnp.where(upper, x, pltpu.roll(x, ROWS - distance, 0)) for x in tiles]
        spot = ((slot_row >> (step + 1)) << level) + (slot_row & (2 * distance - 1))
        tiles = merged(leading, trailing, picked(slot_column == spot, level).astype(jnp.int32), lead_tiles)
    for k, x in enumerate(tiles):
        out[:, tile(k)] = x
    encode(tiles, lead_tiles, words, notes)


def pieces_of(count, lead_tiles):
    starts = [0] + list(range(lead_tiles, count, SET)) + [count]
    return [range(at, to) for at, to in zip(starts[:-1], starts[1:])]


def encode(tiles, lead_tiles, words, notes):
    lane = lanes()
    body = tiles[lead_tiles:]
    for k in range(lead_tiles):
        notes[:, tile(k)] = tiles[k]
    note = jnp.zeros((ROWS, LANES), F32)
    steps = []
    for number, members in enumerate(pieces_of(len(body), lead_tiles)):
        top, bottom = body[members[0]], body[members[0]]
        for k in members[1:]:
            top, bottom = jnp.maximum(top, body[k]), jnp.minimum(bottom, body[k])
        top = jnp.max(top, axis=1, keepdims=True)
        bottom = jnp.min(bottom, axis=1, keepdims=True)
        middle = 0.5 * top + 0.5 * bottom
        half = jnp.maximum(0.5 * top - 0.5 * bottom, 1e-30)
        note = jnp.where(lane == 2 * number, middle, note)
        note = jnp.where(lane == 2 * number + 1, half * (1.0 / LARGEST), note)
        per_step = jnp.broadcast_to(LARGEST / half, (ROWS, LANES))
        middle = jnp.broadcast_to(middle, (ROWS, LANES))
        steps.extend(jnp.floor((body[k] - middle) * per_step + 0.5) for k in members)
    notes[:, tile(lead_tiles)] = note
    if len(steps) % 2:
        steps.append(jnp.zeros((ROWS, LANES), F32))
    for k in range(len(steps) // 2):
        pair = jnp.concatenate([steps[2 * k], steps[2 * k + 1]], axis=0)
        words[:, tile(k)] = pair.astype(jnp.int32).astype(jnp.int16)


def decode(words, notes, count, lead_tiles):
    tiles = [notes[:, tile(k)] for k in range(lead_tiles)]
    note = notes[:, tile(lead_tiles)]
    steps = []
    for k in range(words.shape[1] // LANES):
        pair = words[:, tile(k)].astype(jnp.int32).astype(F32)
        steps += [pair[:ROWS], pair[ROWS:]]
    for number, members in enumerate(pieces_of(count - lead_tiles, lead_tiles)):
        middle = jnp.broadcast_to(note[:, 2 * number : 2 * number + 1], (ROWS, LANES))
        size = jnp.broadcast_to(note[:, 2 * number + 1 : 2 * number + 2], (ROWS, LANES))
        tiles.extend(steps[k] * size + middle for k in members)
    return tiles


def ordered(mine, theirs, is_upper):
    leading = [jnp.where(is_upper, y, x) for x, y in zip(mine, theirs)]
    trailing = [jnp.where(is_upper, x, y) for x, y in zip(mine, theirs)]
    return leading, trailing


def tiles_of(ref):
    return [ref[:, tile(k)] for k in range(ref.shape[1] // LANES)]


def merge_kernel(level, lead_tiles, info, own, words, notes, other, across, shifts, out, *sent):
    mine = tiles_of(own)
    theirs = decode(words, notes, len(mine), lead_tiles)
    if level == 0:
        for k in range(lead_tiles):
            mine[k], theirs[k] = mine[k] + other[:, tile(k)], theirs[k] + across[:, tile(k)]
    tiles = merged(*ordered(mine, theirs, info[2 + level] == 1), shifts[level], lead_tiles)
    for k, x in enumerate(tiles):
        out[:, tile(k)] = x
    if sent:
        encode(tiles, lead_tiles, *sent)


def back_kernel(level, sizes, info, own, words, notes, shifts, weights, spread, dedispersed, scores, steps):
    frames, lead, tail, factor, window_count, stations = sizes
    first, last = info[0] == 0, info[1] == 1
    lead_tiles, main_tiles, tail_tiles = lead // LANES, frames // LANES, tail // LANES
    if level is None:
        series = tiles_of(own)
    else:
        is_upper = info[2 + level] == 1
        mine = tiles_of(own)
        theirs = decode(words, notes, len(mine), lead_tiles)
        series = merged(*ordered(mine, theirs, is_upper), shifts[level], lead_tiles)
    means = [series[k] * (1.0 / window_count) for k in range(lead_tiles)]
    settled = jnp.broadcast_to(means[-1][:, LANES - 1 :], (ROWS, LANES))
    for k in range(main_tiles + tail_tiles):
        mean = jnp.where(first, means[k], settled) if k < lead_tiles else settled
        value = (series[2 * lead_tiles + k] - mean) * factor
        if k < main_tiles:
            dedispersed[:, tile(k)] = value
        else:
            value = jnp.where(last, 0.0, value)
        steps[k * ROWS : (k + 1) * ROWS, :] = value

    reach = tail_tiles + 1
    parts = []
    for q in range(reach):
        parts.append(
            jnp.concatenate([steps[pl.ds(d + ROWS * q, main_tiles, stride=ROWS), :] for d in range(ROWS)], axis=0)
        )
    operand = jnp.concatenate(parts, axis=1)
    high, low = split(operand)
    weight_high, weight_low = split(weights[...])
    product = lax.dot_general(
        jnp.concatenate([weight_high, weight_high, weight_low], axis=1),
        jnp.concatenate([high, low, high], axis=1),
        NT,
        preferred_element_type=F32,
    )
    blocks = LANES // STRIDE
    templates = product.shape[0] // blocks
    sets = product.shape[1] // LANES
    grouped = jnp.concatenate(
        [
            jnp.concatenate([product[i * templates : (i + 1) * templates, tile(a)] for i in range(blocks)], axis=1)
            for a in range(sets)
        ],
        axis=0,
    )
    placed = jnp.dot(jnp.concatenate(split(grouped), axis=0), spread[...], preferred_element_type=F32)
    count = sets * templates
    placed = placed[:count] + placed[count:]
    trials = LANES // main_tiles
    positions = main_tiles * blocks
    for a in range(sets):
        for d in range(trials):
            scores[a * trials + d] = placed[a * templates : (a + 1) * templates, d * positions : (d + 1) * positions]


def swapped(x, axis, distance):
    return lax.ppermute(x, axis, [(i, i ^ distance) for i in range(lax.axis_size(axis))])


def template_weights(tap_index, tap_weight, reach):
    hit = tap_index[:, :, None] == jnp.arange(WIN, dtype=jnp.int32)[None, None, :]
    template = jnp.sum(jnp.where(hit, tap_weight[:, :, None], 0.0), axis=1)
    width = reach * LANES
    rows = [
        jnp.pad(template, ((0, 0), (i * STRIDE, width - WIN - i * STRIDE))) for i in range(LANES // STRIDE)
    ]
    return jnp.concatenate(rows, axis=0)


def wide_merge(own, partner, is_upper, shifts):
    leading = jnp.where(is_upper, partner, own)
    trailing = jnp.where(is_upper, own, partner)
    place = jnp.arange(own.shape[1], dtype=jnp.int32)[None, :] - shifts[:, None]
    picked = jnp.take_along_axis(trailing, jnp.maximum(place, 0), axis=1)
    return leading + jnp.where(place >= 0, picked, 0.0)


def on_device(voltages, pfb_taps, local_shift, cross_shift, tap_index, tap_weight):
    frames, channels = voltages.shape[1:]
    tap_count = pfb_taps.shape[0]
    trials = cross_shift.shape[1]
    local_levels = local_shift.shape[0]
    tm_size, freq_size = lax.axis_size("tm"), lax.axis_size("freq")
    levels = freq_size.bit_length() - 1
    group = channels // trials
    margin = round_up(tap_count, 16)
    cross_reach = sum(trials * 2**level - 1 for level in range(levels))
    lead = round_up(local_levels * (LSHIFT - 1) + cross_reach, LANES)
    tail = round_up(WIN - STRIDE, LANES)

    time, freq = lax.axis_index("tm"), lax.axis_index("freq")
    info = jnp.stack(
        [time, (time == tm_size - 1).astype(jnp.int32)] + [freq >> level & 1 for level in range(max(levels, 1))]
    ).astype(jnp.int32)
    halo_rows = round_up(max(lead + margin, tail), 16)
    if tm_size == 2:
        start = jnp.where(time == 0, frames - halo_rows, 0)
        sent = lax.dynamic_slice_in_dim(voltages, start, halo_rows, axis=1)
        halo = swapped(sent, "tm", 1)
    else:
        raise NotImplementedError("tm")

    chunk_tiles, pieces = 18, 4
    table = jnp.asarray(dft_table(channels, group))
    extended = lead + frames + tail
    width = lead + extended

    sizes = (frames, lead, tail, chunk_tiles, pieces, tap_count) + local_shift.shape
    wide = 2 * channels
    packed = jnp.concatenate([table, jnp.pad(pfb_taps, ((0, 0), (0, wide - channels)))], axis=0)

    def front(*refs):
        front_kernel(sizes, *refs)

    lead_tiles, body_tiles = lead // LANES, extended // LANES
    sent_shapes = (
        jax.ShapeDtypeStruct((2 * ROWS, -(-body_tiles // 2) * LANES), jnp.int16),
        jax.ShapeDtypeStruct((trials, lead + LANES), F32),
    )
    series_shape = jax.ShapeDtypeStruct((trials, width), F32)
    series, *sent = pl.pallas_call(
        front,
        out_shape=(series_shape,) + sent_shapes,
        in_specs=[SMEM, ANY, VMEM, VMEM, VMEM],
        out_specs=(VMEM,) * 3,
        scratch_shapes=[
            pltpu.VMEM(voltages.shape, BF),
            pltpu.VMEM((2, margin + extended, channels), F32),
            *[pltpu.VMEM((chunk_tiles * LANES, channels), F32)] * 4,
            *[pltpu.VMEM((2 * channels, chunk_tiles * LANES), F32)] * 2,
            pltpu.VMEM((trials, width), F32),
            pltpu.VMEM((channels, LANES), F32),
            pltpu.SemaphoreType.DMA((pieces,)),
        ],
        compiler_params=pltpu.CompilerParams(vmem_limit_bytes=52 * 1024 * 1024),
        cost_estimate=pl.CostEstimate(flops=2 * 10**10, bytes_accessed=4096, transcendentals=0),
        name="front",
    )(info, voltages, halo, packed, local_shift)

    shift_rows = jnp.broadcast_to(cross_shift[:, :, None], cross_shift.shape + (LANES,))
    short = [level for level in range(levels) if trials * 2**level <= LANES]
    fused = len(short) == levels > 1
    response = sent[1][:, :lead]
    other = swapped(response, "tm", 1)
    for level in range(levels - 1 if fused else levels):
        if level in short:
            if level == min(1, levels - 2):
                (tap_index, tap_weight), sent = lax.optimization_barrier(((tap_index, tap_weight), sent))
                weights = template_weights(tap_index, tap_weight, tail // LANES + 1)
            received = [swapped(x, "freq", 2**level) for x in sent]
            if level == min(1, levels - 2):
                received[0], weights = lax.optimization_barrier((received[0], weights))
            if level == 0:
                pairs = [(i, i ^ tm_size ^ 1) for i in range(freq_size * tm_size)]
                across = lax.ppermute(response, ("freq", "tm"), pairs)
            shapes = (series_shape,) + (sent_shapes if level + 1 in short else ())

            def merge(*refs, level=level):
                merge_kernel(level, lead_tiles, *refs)

            series, *sent = pl.pallas_call(
                merge,
                out_shape=shapes,
                in_specs=[SMEM] + [VMEM] * 6,
                out_specs=(VMEM,) * len(shapes),
                compiler_params=PARAMS,
                name="merge",
            )(info, series, *received, other, across, shift_rows)
        else:
            partner = swapped(series, "freq", 2**level)
            series = wide_merge(series, partner, info[2 + level] == 1, cross_shift[level])

    if fused:
        last_level = levels - 1
        received = [swapped(x, "freq", 2**last_level) for x in sent]
    else:
        last_level = None
        received = [other, other]

    templates = tap_index.shape[0]
    spread = jnp.asarray(spread_table(frames // LANES, LANES // STRIDE))
    factor = 1.0 / (channels * math.sqrt(channels * freq_size))

    def back(*refs):
        back_kernel(last_level, (frames, lead, tail, factor, frames * tm_size, STRIDE), *refs)

    return pl.pallas_call(
        back,
        out_shape=(
            jax.ShapeDtypeStruct((trials, frames), F32),
            jax.ShapeDtypeStruct((trials, templates, frames // STRIDE), F32),
        ),
        in_specs=[SMEM] + [VMEM] * 6,
        out_specs=(VMEM, VMEM),
        scratch_shapes=[pltpu.VMEM(((frames + tail) // LANES * ROWS + ROWS, LANES), F32)],
        compiler_params=PARAMS,
        name="back",
    )(info, series, *received, shift_rows, weights, spread)


def solution(mesh):
    return jax.shard_map(
        on_device,
        mesh=mesh,
        in_specs=(P("beam", "tm", "freq"), P(), P(None, "freq"), P(None, "freq"), P(), P()),
        out_specs=(P(("beam", "freq"), "tm"), P(("beam", "freq"), None, "tm")),
        check_vma=False,
    )
```
